256 devices in a mesh: row: 64 (over z, x, core), col: 4 (over y).
Axes of the slice: x: 4, y: 4, z: 8, core: 2. Of those that a mesh axis runs over, the one named last changes fastest.
Arguments:
- hamiltonian: bfloat16 [18432, 128, 128], P('row'), may hold values from -0.15625 to 0.15625
- block_column: int32 [18432], P('row'), may hold values from 0 to 1535, as said below
- vectors: bfloat16 [196608, 512], P('row', 'col'), may hold values from -6 to 6
Outputs:
- filtered: bfloat16 [196608, 512], P('row', 'col')
- intersection: float32 [512, 512], P('col')
The draws below stay inside these ranges and needn't reach their ends.
Inputs may be any that keep to these rules, and one draw needn't show every extreme that they name: Block row b's entries are block_column[b * 12 + k]. Entry k = 0 is b itself. Entries k < 10 are distinct and lie among the 24 block rows of b's own index of row (block rows i * 24 to i * 24 + 23 for i = b // 24). For k >= 10, let s = (b % 24) * 2 + k - 10 and g = s // 12; the entry lies among the block rows of index (i + o) mod 64, with o = g + 1 if g < 2, else 2 - 1 - g.
All inputs are finite; a program needn't handle non-finite values.
Results may differ from the reference program's by a relative error of at most 0.0056.
Values may be sent and summed in bfloat16 or wider, within the bound.
A program may use at most 192 MiB of HBM per device.

```python
import jax
import jax.numpy as jnp
from jax import lax

BS = 128
NVEC = 512
RB_DEV = 24
BPR = 12
RPR = 2
REACH = 2
STEPS = 3
CAP = 12
NBR = 1536
NORB = 196608
N_ROW = 64


def draw_block_column(key, part):
    key = jax.random.fold_in(key, 11)
    key_order, key_remote = jax.random.split(key)
    row_inside = jnp.arange(RB_DEV)[None, :, None]
    candidate = jnp.arange(RB_DEV)[None, None, :]
    scores = jax.random.randint(key_order, (N_ROW, RB_DEV, RB_DEV), 0, 1 << 20) * RB_DEV + candidate
    scores = jnp.where(candidate == row_inside, -1, scores)
    order = jnp.argsort(scores, axis=-1, stable=True)
    local_cols = order[:, :, :BPR - RPR]
    remote_pick = jax.random.randint(key_remote, (N_ROW, RB_DEV, RPR), 0, RB_DEV)
    local = jnp.concatenate([local_cols, remote_pick], axis=-1)
    device = jnp.arange(N_ROW)[:, None, None]
    position = jnp.arange(BPR)[None, None, :]
    slot_number = jnp.arange(RB_DEV)[None, :, None] * RPR + position - (BPR - RPR)
    group = jnp.clip(slot_number, 0, 2 * REACH * CAP - 1) // CAP
    offset = jnp.where(group < REACH, group + 1, REACH - 1 - group)
    owner = jnp.where(position < BPR - RPR, device, (device + offset) % N_ROW)
    return (owner * RB_DEV + local).reshape(-1).astype(jnp.int32)


def levels(key, extent, shards, smallest, largest):
    level, own = 1.0, jax.random.fold_in(key, 6)
    for dim, shards_of in shards:
        steps = jnp.exp(jax.random.uniform(jax.random.fold_in(own, dim), (shards_of,), jnp.float32, smallest / len(shards), largest / len(shards)))
        level = level * jnp.repeat(steps, extent[dim] // shards_of).reshape([-1 if axis == dim else 1 for axis in range(len(extent))])
    return level


def normal_values(own_key, dims, spread, limit, cuts=(), dtype=jnp.bfloat16):
    factor_of = levels(own_key, dims, cuts, -0.22, 0.18) if cuts else 1.0
    array = jax.random.normal(own_key, dims, jnp.float32) * spread * factor_of
    return jnp.minimum(jnp.maximum(array, -limit), limit).astype(dtype)


def setup_inputs(seed: int = 0) -> dict:
    key_list = jax.random.split(jax.random.key(seed), 4)
    return {
        "hamiltonian": normal_values(key_list[0], (NBR * BPR, BS, BS), (BPR * BS) ** -0.5, 0.15625, ((0, 64),)),
        "block_column": draw_block_column(jax.random.fold_in(key_list[3], 71), 0),
        "vectors": normal_values(key_list[2], (NORB, NVEC), 1.0, 6.0, ((0, 64), (1, 4))),
    }


filter_center = 0.2
filter_half = 0.8


def operate(hamiltonian, block_column, blocks):
    matrix_rows = hamiltonian.reshape(NBR, BPR, BS, BS)
    column_rows = block_column.reshape(NBR, BPR)

    def one_row(paired):
        row_blocks, row_columns = paired
        gathered = blocks[row_columns].astype(jnp.float32)
        return jnp.einsum("qij,qjk->ik", row_blocks.astype(jnp.float32), gathered)

    return lax.map(one_row, (matrix_rows, column_rows))


def reference(hamiltonian, block_column, vectors):
    previous = vectors.reshape(NBR, BS, NVEC)
    current = ((operate(hamiltonian, block_column, previous) - filter_center * previous.astype(jnp.float32)) / filter_half).astype(jnp.bfloat16)
    for section in range(STEPS - 1):
        product = operate(hamiltonian, block_column, current)
        following = (2.0 * (product - filter_center * current.astype(jnp.float32)) / filter_half - previous.astype(jnp.float32)).astype(jnp.bfloat16)
        previous, current = current, following
    filtered = current.reshape(NORB, NVEC)
    intersection = jnp.dot(filtered.T, filtered, preferred_element_type=jnp.float32) / NORB
    return filtered, intersection
```

```python
import functools

import jax
import jax.numpy as jnp
from jax import lax
from jax.experimental import pallas as pl
from jax.experimental.pallas import tpu as pltpu
from jax.sharding import PartitionSpec as P

MESH = pl.DeviceIdType.MESH
STEPS = 3
OFFSETS = (1, 2, -1, -2)
ORDER = (1, 3, 0, 2)
BF16 = jnp.bfloat16
F32 = jnp.float32
CENTER = 0.2
HALF = 0.8
X = 4
Y = 4


def kernel(
    rows,
    norb,
    bc_s,
    bc_h,
    h_hbm,
    v_hbm,
    f_hbm,
    inter,
    ham,
    vec,
    acc,
    hrem,
    psend,
    precv,
    ridx,
    mine,
    half_recv,
    tsum,
    y_recv,
    usum,
    x_recv,
    zsum,
    z_recv,
    final,
    every,
    ssum,
    load_sem,
    idx_sem,
    h_sem,
    fwd_sem,
    p_sem,
    a_sem,
    s_sem,
    out_sem,
):
    z_count = rows // (2 * X)
    r = lax.axis_index("row")
    y = lax.axis_index("col")
    core = lax.rem(r, 2)
    x = lax.rem(r // 2, X)
    z = r // (2 * X)
    bs = ham.shape[-1]
    quarter, eighth = bs // 4, bs // 8
    base = r * 24

    def inside(entry):
        return jnp.clip(entry - base, 0, 23)

    def row_at(offset):
        return lax.rem(r + offset + rows, rows)

    def col_at(offset):
        return lax.rem(y + offset + Y, Y)

    def x_at(offset, c):
        return z * 2 * X + lax.rem(x + offset, X) * 2 + c

    def z_at(offset):
        return lax.rem(z + offset, z_count) * 2 * X + x * 2 + core

    loads = [pltpu.make_async_copy(v_hbm, vec.at[0], load_sem.at[4])]
    loads += [
        pltpu.make_async_copy(
            h_hbm.at[pl.ds(6 * g, 6)], ham.at[pl.ds(6 * g, 6)], load_sem.at[g]
        )
        for g in range(4)
    ]
    for load in loads:
        load.start()

    peers = [(row_at(o), y) for o in OFFSETS]
    peers += [(r, col_at(d)) for d in range(1, Y)]
    peers += [(x_at(d, c), y) for d in range(1, X) for c in range(2)]
    peers += [(z_at(d), y) for d in range(1, z_count)]
    barrier = pltpu.get_barrier_semaphore()
    for peer in peers:
        pl.semaphore_signal(barrier, inc=1, device_id=peer, device_id_type=MESH)
    pl.semaphore_wait(barrier, len(peers))

    def remote(src, dst, send, recv, peer):
        return pltpu.make_async_remote_copy(
            src_ref=src,
            dst_ref=dst,
            send_sem=send,
            recv_sem=recv,
            device_id=peer,
            device_id_type=MESH,
        )

    g_x_out, g_chip_out = 2 * (1 - core), 2 * core
    g_x_in, g_chip_in = 2 * core, 2 * (1 - core)
    to_row = (row_at(2), row_at(-2), lax.rem(r + 2 * core - 1 + rows, rows))
    partner = r + 1 - 2 * core
    out_group = (1, 3, g_x_out)
    in_group = (1, 3, g_x_in)

    def rows_of(part, size):
        return pl.ds(pl.multiple_of(part * size, size), size)

    h_copies = []
    for j in range(3):
        g = out_group[j]
        copy = remote(
            h_hbm.at[pl.ds(6 * g, 6), pl.ds(10, 2), rows_of(y, quarter)],
            hrem.at[g, :, :, rows_of(y, quarter)],
            h_sem.at[0, j],
            h_sem.at[1, j],
            (to_row[j], y),
        )
        copy.start()
        h_copies.append(copy)
    idx_copies = []
    for g in range(4):
        copy = remote(
            bc_h, ridx.at[g], idx_sem.at[0, g], idx_sem.at[1, g], (row_at(OFFSETS[g]), y)
        )
        copy.start()
        idx_copies.append(copy)
    chip_copy = remote(
        h_hbm.at[pl.ds(6 * g_chip_out, 6), pl.ds(10, 2)],
        hrem.at[g_chip_out],
        h_sem.at[0, 3],
        h_sem.at[1, 3],
        (partner, y),
    )
    chip_copy.start()

    def local_rows(current, first_row, count):
        def body(i, carry):
            b = first_row + i
            lhs = jnp.concatenate([ham[b, k] for k in range(10)], axis=1)
            rhs = jnp.concatenate(
                [vec[current, inside(bc_s[b * 12 + k])] for k in range(10)], axis=0
            )
            acc[b] = jnp.dot(lhs, rhs, preferred_element_type=F32)
            return carry

        lax.fori_loop(0, count, body, 0, unroll=2)

    def products(step, g):
        def body(i, carry):
            lhs = jnp.concatenate([hrem[g, i, 0], hrem[g, i, 1]], axis=1)
            rhs = jnp.concatenate(
                [
                    vec[step, inside(ridx[g, (6 * g + i) * 12 + 10 + q])]
                    for q in range(2)
                ],
                axis=0,
            )
            psend[step, g, i] = jnp.dot(lhs, rhs, preferred_element_type=F32).astype(BF16)
            return carry

        lax.fori_loop(0, 6, body, 0, unroll=2)

    def send_products(step, g):
        copy = remote(
            psend.at[step, g],
            precv.at[step, g],
            p_sem.at[0, step, g],
            p_sem.at[1, step, g],
            (row_at(-OFFSETS[g]), y),
        )
        copy.start()
        return copy

    loads[0].wait()
    loads[1].wait()
    local_rows(0, 0, 6)

    fwd = []
    for j in range(3):
        h_copies[j].wait_recv()
        part = hrem.at[in_group[j], :, :, rows_of(y, quarter)]
        pair = []
        for side, d in enumerate((1, -1)):
            copy = remote(
                part, part, fwd_sem.at[0, j, side], fwd_sem.at[1, j, side], (r, col_at(d))
            )
            copy.start()
            pair.append(copy)
        fwd.append(pair)

    loads[2].wait()
    local_rows(0, 6, 6)

    second = []
    for j in range(3):
        pair = []
        for side, d in enumerate((1, -1)):
            fwd[j][side].wait_recv()
            part = hrem.at[
                in_group[j], :, :, rows_of(col_at(-d) * 2 + side, eighth)
            ]
            copy = remote(
                part, part, fwd_sem.at[0, j, 2 + side], fwd_sem.at[1, j, 2 + side], (r, col_at(d))
            )
            copy.start()
            pair.append(copy)
        second.append(pair)

    loads[3].wait()
    local_rows(0, 12, 6)
    loads[4].wait()
    local_rows(0, 18, 6)

    for copy in idx_copies:
        copy.wait_recv()

    p_copies = []

    def finish(step, g, copy):
        copy.wait_recv()

        def body(i, carry):
            b = 6 * g + i
            product = acc[b] + precv[step, g, i].astype(F32)
            shifted = product - CENTER * vec[step, b].astype(F32)
            if step == 0:
                vec[1, b] = (shifted / HALF).astype(BF16)
            else:
                vec[step + 1, b] = (
                    2.0 * shifted / HALF - vec[step - 1, b].astype(F32)
                ).astype(BF16)
            return carry

        lax.fori_loop(0, 6, body, 0, unroll=2)

    def receive(step, g):
        return remote(
            psend.at[step, g], precv.at[step, g], p_sem.at[0, step, g], p_sem.at[1, step, g], (r, y)
        )

    arrival = (g_chip_out, 1, 3, g_x_out)
    for step in range(STEPS):
        if step == 0:
            for j in range(3):
                for copy in second[j]:
                    copy.wait_recv()
                g = in_group[j]
                products(0, g)
                o = OFFSETS[g] if j < 2 else 1 - 2 * core
                copy = remote(
                    psend.at[0, g],
                    precv.at[0, g],
                    p_sem.at[0, 0, g],
                    p_sem.at[1, 0, g],
                    (row_at(-o), y),
                )
                copy.start()
                p_copies.append(copy)
            chip_copy.wait_recv()
            products(0, g_chip_in)
            copy = remote(
                psend.at[0, g_chip_in],
                precv.at[0, g_chip_in],
                p_sem.at[0, 0, g_chip_in],
                p_sem.at[1, 0, g_chip_in],
                (partner, y),
            )
            copy.start()
            p_copies.append(copy)
        else:
            for g in ORDER:
                products(step, g)
                p_copies.append(send_products(step, g))
            local_rows(step, 0, 24)
        for g in arrival:
            finish(step, g, receive(step, g))
            if step == STEPS - 1:

                @pl.when(g != y)
                def _():
                    remote(
                        vec.at[STEPS, pl.ds(6 * g, 6)],
                        mine.at[y],
                        a_sem.at[0, g],
                        a_sem.at[1, y],
                        (r, g),
                    ).start()

                @pl.when(g == y)
                def _():
                    pltpu.make_async_copy(
                        vec.at[STEPS, pl.ds(6 * g, 6)], mine.at[y], a_sem.at[1, y]
                    ).start()

                pltpu.make_async_copy(
                    vec.at[STEPS, pl.ds(6 * g, 6)],
                    f_hbm.at[pl.ds(6 * g, 6)],
                    out_sem.at[g],
                ).start()

    pltpu.make_async_copy(
        vec.at[STEPS, pl.ds(6 * y, 6)], mine.at[y], a_sem.at[1, y]
    ).wait()
    for d in range(1, Y):
        s = col_at(d)
        remote(
            vec.at[STEPS, pl.ds(6 * s, 6)], mine.at[s], a_sem.at[0, s], a_sem.at[1, s], (r, s)
        ).wait_recv()

    depth = 6 * bs
    everything = jnp.concatenate(
        [mine[s].reshape(depth, bs) for s in range(Y)], axis=1
    )

    for i in range(Y):
        part = lax.dot_general(
            mine[i].reshape(depth, bs),
            everything,
            (((0,), (0,)), ((), ())),
            preferred_element_type=F32,
        )
        for c in range(2):
            ssum[c, i] = part[:, c * 2 * bs : (c + 1) * 2 * bs].astype(BF16)

    copy_c = remote(
        ssum.at[1 - core], half_recv, s_sem.at[0, 0], s_sem.at[1, 0], (partner, y)
    )
    copy_c.start()
    copy_c.wait_recv()
    for i in range(Y):
        tsum[i] = (ssum[core, i].astype(F32) + half_recv[i].astype(F32)).astype(BF16)

    y_copies = []
    for d in range(1, Y):
        s = col_at(d)
        copy = remote(
            tsum.at[s], y_recv.at[Y - d], s_sem.at[0, d], s_sem.at[1, d], (r, s)
        )
        copy.start()
        y_copies.append(copy)
    total = tsum[y].astype(F32)
    for d in range(1, Y):
        y_copies[d - 1].wait_recv()
    for d in range(1, Y):
        total += y_recv[d].astype(F32)
    for i in range(X):
        usum[i] = total[i * quarter : (i + 1) * quarter].astype(BF16)

    x_copies = []
    for d in range(1, X):
        copy = remote(
            usum.at[lax.rem(x + d, X)],
            x_recv.at[X - d],
            s_sem.at[0, 3 + d],
            s_sem.at[1, 3 + d],
            (x_at(d, core), y),
        )
        copy.start()
        x_copies.append(copy)
    total = usum[x].astype(F32)
    for d in range(1, X):
        x_copies[d - 1].wait_recv()
    for d in range(1, X):
        total += x_recv[d].astype(F32)
    zsum[...] = total.astype(BF16)

    z_copies = []
    for d in range(1, z_count):
        copy = remote(
            zsum,
            z_recv.at[z_count - d],
            s_sem.at[0, 6 + d],
            s_sem.at[1, 6 + d],
            (z_at(d), y),
        )
        copy.start()
        z_copies.append(copy)
    total = zsum[...].astype(F32)
    for copy in z_copies:
        copy.wait_recv()
    for d in range(1, z_count):
        total += z_recv[d].astype(F32)
    final[...] = total / norb

    last = []
    for d in range(X):
        for e in range(2):
            if d == 0 and e == 0:
                continue
            n = 14 + 2 * d + e
            copy = remote(
                final,
                every.at[X - d if d else 0, e],
                s_sem.at[0, n],
                s_sem.at[1, n],
                (x_at(d, lax.rem(core + e, 2)), y),
            )
            copy.start()
            last.append(copy)

    def place(xx, c, value):
        inter[rows_of(xx, quarter), pl.ds(pl.multiple_of(c * 2 * bs, 2 * bs), 2 * bs)] = value

    place(x, core, final[...])
    for copy in last:
        copy.wait_recv()
    for d in range(X):
        for e in range(2):
            if d == 0 and e == 0:
                continue
            place(
                lax.rem(x + (X - d), X),
                lax.rem(core + e, 2),
                every[X - d if d else 0, e],
            )

    for group in ([chip_copy], h_copies, idx_copies, p_copies, y_copies, x_copies, z_copies, last, [copy_c]):
        for copy in group:
            copy.wait_send()
    for pair in fwd + second:
        for copy in pair:
            copy.wait_send()
    for d in range(1, Y):
        s = col_at(d)
        remote(
            vec.at[STEPS, pl.ds(6 * s, 6)], mine.at[y], a_sem.at[0, s], a_sem.at[1, y], (r, s)
        ).wait_send()
    for g in range(4):
        pltpu.make_async_copy(
            vec.at[STEPS, pl.ds(6 * g, 6)], f_hbm.at[pl.ds(6 * g, 6)], out_sem.at[g]
        ).wait()


def on_device(hamiltonian, block_column, vectors):
    bs = hamiltonian.shape[1]
    rows = lax.axis_size("row")
    z_count = rows // (2 * X)
    ham = hamiltonian.reshape(24, 12, bs, bs)
    vec = vectors.reshape(24, bs, bs)
    dma = pltpu.SemaphoreType.DMA
    any_spec = pl.BlockSpec(memory_space=pl.ANY)
    filtered, inter = pl.pallas_call(
        functools.partial(kernel, rows, float(rows * 24 * bs)),
        out_shape=(
            jax.ShapeDtypeStruct((24, bs, bs), BF16),
            jax.ShapeDtypeStruct((bs, Y * bs), F32),
        ),
        in_specs=[pl.BlockSpec(memory_space=pltpu.SMEM), any_spec, any_spec, any_spec],
        out_specs=(any_spec, pl.BlockSpec(memory_space=pltpu.VMEM)),
        scratch_shapes=[
            pltpu.VMEM((24, 12, bs, bs), BF16),
            pltpu.VMEM((STEPS + 1, 24, bs, bs), BF16),
            pltpu.VMEM((24, bs, bs), F32),
            pltpu.VMEM((4, 6, 2, bs, bs), BF16),
            pltpu.VMEM((STEPS, 4, 6, bs, bs), BF16),
            pltpu.VMEM((STEPS, 4, 6, bs, bs), BF16),
            pltpu.SMEM((4, 288), jnp.int32),
            pltpu.VMEM((Y, 6, bs, bs), BF16),
            pltpu.VMEM((Y, bs, 2 * bs), BF16),
            pltpu.VMEM((Y, bs, 2 * bs), BF16),
            pltpu.VMEM((Y, bs, 2 * bs), BF16),
            pltpu.VMEM((X, bs // 4, 2 * bs), BF16),
            pltpu.VMEM((X, bs // 4, 2 * bs), BF16),
            pltpu.VMEM((bs // 4, 2 * bs), BF16),
            pltpu.VMEM((z_count, bs // 4, 2 * bs), BF16),
            pltpu.VMEM((bs // 4, 2 * bs), F32),
            pltpu.VMEM((X, 2, bs // 4, 2 * bs), F32),
            pltpu.VMEM((2, Y, bs, 2 * bs), BF16),
            dma((5,)),
            dma((2, 4)),
            dma((2, 4)),
            dma((2, 3, 4)),
            dma((2, STEPS, 4)),
            dma((2, 4)),
            dma((2, 22)),
            dma((4,)),
        ],
        compiler_params=pltpu.CompilerParams(
            collective_id=0, has_side_effects=True, vmem_limit_bytes=50 * 2**20
        ),
        name="chebyshev",
    )(block_column, block_column, ham, vec)
    return filtered.reshape(24 * bs, bs), inter


def solution(mesh):
    return jax.shard_map(
        on_device,
        mesh=mesh,
        in_specs=(P("row", None, None), P("row"), P("row", "col")),
        out_specs=(P("row", "col"), P("col", None)),
        check_vma=False,
    )
```

```python
import functools

import jax
import jax.numpy as jnp
from jax import lax
from jax.experimental import pallas as pl
from jax.experimental.pallas import tpu as pltpu
from jax.sharding import PartitionSpec as P

MESH = pl.DeviceIdType.MESH
STEPS = 3
OFFSETS = (1, 2, -1, -2)
BF16 = jnp.bfloat16
F32 = jnp.float32
CENTER = 0.2
HALF = 0.8
X = 4
Y = 4
PARTS = 3
PER_PART = 6 // PARTS


def kernel(
    rows,
    norb,
    bc_s,
    bc_h,
    h_hbm,
    v_hbm,
    f_hbm,
    inter,
    ham,
    vec,
    acc,
    hrem,
    psend,
    precv,
    ridx,
    mine,
    half_recv,
    tsum,
    y_recv,
    usum,
    x_recv,
    zsum,
    z_recv,
    final,
    every,
    ssum,
    load_sem,
    idx_sem,
    h_sem,
    fwd_sem,
    p_sem,
    a_sem,
    s_sem,
    out_sem,
):
    z_count = rows // (2 * X)
    r = lax.axis_index("row")
    y = lax.axis_index("col")
    core = lax.rem(r, 2)
    x = lax.rem(r // 2, X)
    z = r // (2 * X)
    bs = ham.shape[-1]
    piece = bs // (2 * X)
    base = r * 24

    def inside(entry):
        return jnp.clip(entry - base, 0, 23)

    def row_at(offset):
        return lax.rem(r + offset + rows, rows)

    def col_at(offset):
        return lax.rem(y + offset + Y, Y)

    def x_at(offset, c):
        return z * 2 * X + lax.rem(x + offset, X) * 2 + c

    def z_at(offset):
        return lax.rem(z + offset, z_count) * 2 * X + x * 2 + core

    sends = []
    loads = {}

    def load(name, src, dst, sem):
        loads[name] = pltpu.make_async_copy(src, dst, sem)
        loads[name].start()

    def loaded(name):
        loads.pop(name).wait()

    def remote(src, dst, send_sem, recv_sem, peer):
        return pltpu.make_async_remote_copy(
            src_ref=src,
            dst_ref=dst,
            send_sem=send_sem,
            recv_sem=recv_sem,
            device_id=peer,
            device_id_type=MESH,
        )

    def send(*args):
        copy = remote(*args)
        copy.start()
        sends.append(copy)
        return copy

    def close():
        for copy in sends:
            copy.wait_send()
        for name in tuple(loads):
            loaded(name)

    load("vec", v_hbm, vec.at[0], load_sem.at[4])

    def load_rows(g):
        load(g, h_hbm.at[pl.ds(6 * g, 6)], ham.at[pl.ds(6 * g, 6)], load_sem.at[g])

    load_rows(0)

    peers = [(row_at(o), y) for o in OFFSETS]
    peers += [(r, col_at(d)) for d in range(1, Y)]
    peers += [(x_at(d, c), y) for d in range(1, X) for c in range(2)]
    peers += [(z_at(d), y) for d in range(1, z_count)]
    barrier = pltpu.get_barrier_semaphore()
    for peer in peers:
        pl.semaphore_signal(barrier, inc=1, device_id=peer, device_id_type=MESH)
    pl.semaphore_wait(barrier, len(peers))

    g_x_out, g_chip_out = 2 * (1 - core), 2 * core
    g_x_in, g_chip_in = 2 * core, 2 * (1 - core)
    to_row = (row_at(2), row_at(-2), lax.rem(r + 2 * core - 1 + rows, rows))
    partner = r + 1 - 2 * core
    out_group = (1, 3, g_x_out)
    in_group = (1, 3, g_x_in)

    def coupled_hbm(g, first, count):
        return h_hbm.at[pl.ds(6 * g + first, count), pl.ds(10, 2)]

    quarter_copies = [
        send(
            coupled_hbm(g, y, 1),
            hrem.at[g, pl.ds(y, 1)],
            h_sem.at[0, j],
            h_sem.at[1, j],
            (to_row[j], y),
        )
        for j, g in enumerate(out_group)
    ]
    chip_copy = send(
        h_hbm.at[pl.ds(6 * g_chip_out, 6), pl.ds(10, 2)],
        hrem.at[g_chip_out],
        h_sem.at[0, 3],
        h_sem.at[1, 3],
        (partner, y),
    )
    idx_copies = [
        send(bc_h, ridx.at[g], idx_sem.at[0, g], idx_sem.at[1, g], (row_at(OFFSETS[g]), y))
        for g in range(4)
    ]
    lower_copies = [
        send(
            coupled_hbm(g, Y, 2),
            hrem.at[g, pl.ds(Y, 2)],
            h_sem.at[0, 4 + j],
            h_sem.at[1, 4 + j],
            (to_row[j], y),
        )
        for j, g in enumerate(out_group)
    ]

    for g in range(1, 4):
        load_rows(g)

    def local_rows(current, first_row, count, unroll):
        def body(i, carry):
            b = first_row + i
            lhs = jnp.concatenate([ham[b, k] for k in range(10)], axis=1)
            rhs = jnp.concatenate(
                [vec[current, inside(bc_s[b * 12 + k])] for k in range(10)], axis=0
            )
            acc[b] = jnp.dot(lhs, rhs, preferred_element_type=F32)
            return carry

        lax.fori_loop(0, count, body, 0, unroll=unroll)

    def products(step, g):
        def body(i, carry):
            lhs = jnp.concatenate([hrem[g, i, 0], hrem[g, i, 1]], axis=1)
            rhs = jnp.concatenate(
                [
                    vec[step, inside(ridx[g, (6 * g + i) * 12 + 10 + q])]
                    for q in range(2)
                ],
                axis=0,
            )
            psend[step, g, i] = jnp.dot(lhs, rhs, preferred_element_type=F32).astype(BF16)
            return carry

        lax.fori_loop(0, 6, body, 0, unroll=6)

    in_groups = (*in_group, g_chip_in)
    back_to = (row_at(-2), row_at(2), lax.rem(r + 2 * core - 1 + rows, rows), partner)

    def product_copy(step, g, h, peer):
        part = pl.ds(PER_PART * h, PER_PART)
        return (
            psend.at[step, g, part],
            precv.at[step, g, part],
            p_sem.at[0, step, h, g],
            p_sem.at[1, step, h, g],
            peer,
        )

    def send_products(step, j, h):
        send(*product_copy(step, in_groups[j], h, (back_to[j], y)))

    loaded("vec")
    loaded(0)
    local_rows(0, 0, 6, 6)

    fwd = []
    for j in range(3):
        quarter_copies[j].wait_recv()
        part = hrem.at[in_group[j], pl.ds(y, 1)]
        fwd.append(
            [
                send(
                    part,
                    part,
                    fwd_sem.at[0, j, side],
                    fwd_sem.at[1, j, side],
                    (r, col_at(d)),
                )
                for side, d in enumerate((1, -1))
            ]
        )

    loaded(1)
    local_rows(0, 6, 6, 6)

    second = []
    for j in range(3):
        pair = []
        for side, d in enumerate((1, -1)):
            fwd[j][side].wait_recv()
            part = hrem.at[in_group[j], pl.ds(col_at(-d), 1), pl.ds(side, 1)]
            pair.append(
                send(
                    part,
                    part,
                    fwd_sem.at[0, j, 2 + side],
                    fwd_sem.at[1, j, 2 + side],
                    (r, col_at(d)),
                )
            )
        second.append(pair)
        if j < 2:
            loaded(2 + j)
            local_rows(0, 12 + 6 * j, 6, 6)

    for copy in idx_copies:
        copy.wait_recv()


    def finish(step, g, h):
        remote(*product_copy(step, g, h, (partner, y))).wait_recv()

        def body(i, carry):
            b = 6 * g + PER_PART * h + i
            product = acc[b] + precv[step, g, PER_PART * h + i].astype(F32)
            shifted = product - CENTER * vec[step, b].astype(F32)
            if step == 0:
                vec[1, b] = (shifted / HALF).astype(BF16)
            else:
                vec[step + 1, b] = (
                    2.0 * shifted / HALF - vec[step - 1, b].astype(F32)
                ).astype(BF16)
            return carry

        lax.fori_loop(0, PER_PART, body, 0, unroll=PER_PART)

    def to_mine(g, h, source=y, local=False):
        group = vec.at[STEPS, pl.ds(6 * g + PER_PART * h, PER_PART)]
        place = mine.at[source, pl.ds(PER_PART * h, PER_PART)]
        if local:
            return pltpu.make_async_copy(group, place, a_sem.at[1, h, y])
        return remote(group, place, a_sem.at[0, h, g], a_sem.at[1, h, source], (r, g))

    def to_hbm(g, h):
        rows_g = pl.ds(6 * g + PER_PART * h, PER_PART)
        return pltpu.make_async_copy(
            vec.at[STEPS, rows_g], f_hbm.at[rows_g], out_sem.at[h, g]
        )

    def scatter(g, h):
        @pl.when(g != y)
        def _():
            to_mine(g, h).start()

        @pl.when(g == y)
        def _():
            to_mine(g, h, local=True).start()

        to_hbm(g, h).start()

    def close_scatter():
        for h in range(PARTS):
            for d in range(1, Y):
                to_mine(col_at(d), h).wait_send()
            for g in range(4):
                to_hbm(g, h).wait()

    own_groups = (1, 3, g_x_out)
    parts = range(PARTS)
    for step in range(STEPS):

        def complete(g, h, step=step):
            finish(step, g, h)
            if step == STEPS - 1:
                scatter(g, h)

        if step == 0:
            for j in range(3):
                for copy in (*second[j], lower_copies[j]):
                    copy.wait_recv()
                products(0, in_groups[j])
                for h in parts:
                    send_products(0, j, h)
            chip_copy.wait_recv()
            products(0, g_chip_in)
            for h in parts:
                send_products(0, 3, h)
        else:
            for j in (0, 1):
                products(step, in_groups[j])
                send_products(step, j, 0)
            products(step, g_chip_in)
            for h in parts:
                send_products(step, 3, h)
            products(step, in_groups[2])
            send_products(step, 2, 0)
            for h in parts[1:]:
                for j in range(3):
                    send_products(step, j, h)
            local_rows(step, 6 * g_chip_out, 6, 6)
        for h in parts:
            complete(g_chip_out, h)
        if step > 0:
            for g in own_groups:
                local_rows(step, 6 * g, 6, 6)
        for h in parts:
            for g in own_groups:
                complete(g, h)

    for h in parts:
        to_mine(y, h, local=True).wait()
        for d in range(1, Y):
            to_mine(col_at(d), h, source=col_at(d)).wait_recv()

    depth = 6 * bs
    everything = jnp.concatenate(
        [mine[s].reshape(depth, bs) for s in range(Y)], axis=1
    )

    for i in range(Y):
        part = lax.dot_general(
            mine[i].reshape(depth, bs),
            everything,
            (((0,), (0,)), ((), ())),
            preferred_element_type=F32,
        )
        for k in range(2):
            rows_k = slice(k * bs // 2, (k + 1) * bs // 2)
            for c in range(2):
                ssum[k, c, i] = part[rows_k, c * 2 * bs : (c + 1) * 2 * bs].astype(BF16)

    def sem(k, n):
        return s_sem.at[0, k, n], s_sem.at[1, k, n]

    chunks = range(2)
    copies = [
        send(ssum.at[k, 1 - core], half_recv.at[k], *sem(k, 0), (partner, y))
        for k in chunks
    ]
    after = []
    for k in chunks:
        copies[k].wait_recv()
        for i in range(Y):
            both = ssum[k, core, i].astype(F32) + half_recv[k, i].astype(F32)
            tsum[k, i] = both.astype(BF16)
        after.append(
            [
                send(tsum.at[k, col_at(d)], y_recv.at[k, Y - d], *sem(k, d), (r, col_at(d)))
                for d in range(1, Y)
            ]
        )
    copies, after = after, []
    for k in chunks:
        total = tsum[k, y].astype(F32)
        for copy in copies[k]:
            copy.wait_recv()
        for d in range(1, Y):
            total += y_recv[k, d].astype(F32)
        for i in range(X):
            usum[k, i] = total[i * piece : (i + 1) * piece].astype(BF16)
        after.append(
            [
                send(
                    usum.at[k, lax.rem(x + d, X)],
                    x_recv.at[k, X - d],
                    *sem(k, 3 + d),
                    (x_at(d, core), y),
                )
                for d in range(1, X)
            ]
        )
    copies, after = after, []
    for k in chunks:
        total = usum[k, x].astype(F32)
        for copy in copies[k]:
            copy.wait_recv()
        for d in range(1, X):
            total += x_recv[k, d].astype(F32)
        zsum[k] = total.astype(BF16)
        after.append(
            [
                send(zsum.at[k], z_recv.at[k, z], *sem(k, 6 + d), (z_at(d), y))
                for d in range(1, z_count)
            ]
        )
        z_recv[k, z] = total.astype(BF16)
    copies, after = after, []
    others = [(d, e) for d in range(X) for e in range(2) if d or e]
    for k in chunks:
        for copy in copies[k]:
            copy.wait_recv()
        total = z_recv[k, 0].astype(F32)
        for d in range(1, z_count):
            total += z_recv[k, d].astype(F32)
        final[k] = (total / norb).astype(BF16)
        after.append(
            [
                send(
                    final.at[k],
                    every.at[k, X - d if d else 0, e],
                    *sem(k, 14 + 2 * d + e),
                    (x_at(d, lax.rem(core + e, 2)), y),
                )
                for d, e in others
            ]
        )

    def place(k, xx, c, value):
        rows_k = pl.ds(pl.multiple_of(k * bs // 2 + xx * piece, piece), piece)
        columns_c = pl.ds(pl.multiple_of(c * 2 * bs, 2 * bs), 2 * bs)
        inter[rows_k, columns_c] = value.astype(F32)

    for k in chunks:
        place(k, x, core, final[k])
    for k in chunks:
        for copy in after[k]:
            copy.wait_recv()
        for d, e in others:
            back = X - d if d else 0
            place(k, lax.rem(x + back, X), lax.rem(core + e, 2), every[k, back, e])
    close()
    close_scatter()


def on_device(hamiltonian, block_column, vectors):
    bs = hamiltonian.shape[1]
    rows = lax.axis_size("row")
    z_count = rows // (2 * X)
    ham = hamiltonian.reshape(24, 12, bs, bs)
    vec = vectors.reshape(24, bs, bs)
    dma = pltpu.SemaphoreType.DMA
    any_spec = pl.BlockSpec(memory_space=pl.ANY)
    filtered, inter = pl.pallas_call(
        functools.partial(kernel, rows, float(rows * 24 * bs)),
        out_shape=(
            jax.ShapeDtypeStruct((24, bs, bs), BF16),
            jax.ShapeDtypeStruct((bs, Y * bs), F32),
        ),
        in_specs=[pl.BlockSpec(memory_space=pltpu.SMEM), any_spec, any_spec, any_spec],
        out_specs=(any_spec, pl.BlockSpec(memory_space=pltpu.VMEM)),
        scratch_shapes=[
            pltpu.VMEM((24, 12, bs, bs), BF16),
            pltpu.VMEM((STEPS + 1, 24, bs, bs), BF16),
            pltpu.VMEM((24, bs, bs), F32),
            pltpu.VMEM((4, 6, 2, bs, bs), BF16),
            pltpu.VMEM((STEPS, 4, 6, bs, bs), BF16),
            pltpu.VMEM((STEPS, 4, 6, bs, bs), BF16),
            pltpu.SMEM((4, 288), jnp.int32),
            pltpu.VMEM((Y, 6, bs, bs), BF16),
            pltpu.VMEM((2, Y, bs // 2, 2 * bs), BF16),
            pltpu.VMEM((2, Y, bs // 2, 2 * bs), BF16),
            pltpu.VMEM((2, Y, bs // 2, 2 * bs), BF16),
            pltpu.VMEM((2, X, bs // (2 * X), 2 * bs), BF16),
            pltpu.VMEM((2, X, bs // (2 * X), 2 * bs), BF16),
            pltpu.VMEM((2, bs // (2 * X), 2 * bs), BF16),
            pltpu.VMEM((2, z_count, bs // (2 * X), 2 * bs), BF16),
            pltpu.VMEM((2, bs // (2 * X), 2 * bs), BF16),
            pltpu.VMEM((2, X, 2, bs // (2 * X), 2 * bs), BF16),
            pltpu.VMEM((2, 2, Y, bs // 2, 2 * bs), BF16),
            dma((5,)),
            dma((2, 4)),
            dma((2, 7)),
            dma((2, 3, 4)),
            dma((2, STEPS, PARTS, 4)),
            dma((2, PARTS, 4)),
            dma((2, 2, 22)),
            dma((PARTS, 4)),
        ],
        compiler_params=pltpu.CompilerParams(
            collective_id=0, has_side_effects=True, vmem_limit_bytes=64 * 2**20 - 2**17
        ),
        name="chebyshev",
    )(block_column, block_column, ham, vec)
    return filtered.reshape(24 * bs, bs), inter


def solution(mesh):
    return jax.shard_map(
        on_device,
        mesh=mesh,
        in_specs=(P("row", None, None), P("row"), P("row", "col")),
        out_specs=(P("row", "col"), P("col", None)),
        check_vma=False,
    )
```

```python
import functools

import jax
import jax.numpy as jnp
from jax import lax
from jax.experimental import pallas as pl
from jax.experimental.pallas import tpu as pltpu
from jax.sharding import PartitionSpec as P

MESH = pl.DeviceIdType.MESH
STEPS = 3
OFFSETS = (1, 2, -1, -2)
BF16 = jnp.bfloat16
F32 = jnp.float32
CENTER = 0.2
HALF = 0.8
X = 4
Y = 4
PARTS = 3
PER_PART = 6 // PARTS


def kernel(
    rows,
    norb,
    bc_s,
    bc_h,
    h_hbm,
    v_hbm,
    f_hbm,
    inter,
    ham,
    vec,
    acc,
    hrem,
    vsend,
    vrecv,
    psend,
    precv,
    ridx,
    mine,
    half_recv,
    tsum,
    yx_recv,
    zsum,
    z_recv,
    final,
    every,
    ssum,
    load_sem,
    idx_sem,
    h_sem,
    fwd_sem,
    v_sem,
    p_sem,
    a_sem,
    s_sem,
    out_sem,
):
    z_count = rows // (2 * X)
    r = lax.axis_index("row")
    y = lax.axis_index("col")
    core = lax.rem(r, 2)
    x = lax.rem(r // 2, X)
    z = r // (2 * X)
    bs = ham.shape[-1]
    piece = bs // (2 * X)
    base = r * 24

    def inside(entry):
        return jnp.clip(entry - base, 0, 23)

    def row_at(offset):
        return lax.rem(r + offset + rows, rows)

    def col_at(offset):
        return lax.rem(y + offset + Y, Y)

    def x_at(offset, c):
        return z * 2 * X + lax.rem(x + offset, X) * 2 + c

    def z_at(offset):
        return lax.rem(z + offset, z_count) * 2 * X + x * 2 + core

    sends = []
    loads = {}

    def load(name, src, dst, sem):
        loads[name] = pltpu.make_async_copy(src, dst, sem)
        loads[name].start()

    def loaded(name):
        loads.pop(name).wait()

    def remote(src, dst, send_sem, recv_sem, peer):
        return pltpu.make_async_remote_copy(
            src_ref=src,
            dst_ref=dst,
            send_sem=send_sem,
            recv_sem=recv_sem,
            device_id=peer,
            device_id_type=MESH,
        )

    def send(*args):
        copy = remote(*args)
        copy.start()
        sends.append(copy)
        return copy

    def close():
        for copy in sends:
            copy.wait_send()
        for name in tuple(loads):
            loaded(name)

    load("vec", v_hbm, vec.at[0], load_sem.at[4])

    def load_rows(g):
        load(g, h_hbm.at[pl.ds(6 * g, 6)], ham.at[pl.ds(6 * g, 6)], load_sem.at[g])

    load_rows(0)

    peers = [(row_at(o), y) for o in OFFSETS]
    peers += [(r, col_at(d)) for d in range(1, Y)]
    peers += [(x_at(d, c), y) for d in range(1, X) for c in range(2)]
    peers += [(z_at(d), y) for d in range(1, z_count)]
    peers += [(x_at(d, core), col_at(e)) for d in range(1, X) for e in range(1, Y)]
    barrier = pltpu.get_barrier_semaphore()
    for peer in peers:
        pl.semaphore_signal(barrier, inc=1, device_id=peer, device_id_type=MESH)
    pl.semaphore_wait(barrier, len(peers))

    g_x_out, g_chip_out = 2 * (1 - core), 2 * core
    g_x_in, g_chip_in = 2 * core, 2 * (1 - core)
    to_row = (row_at(2), row_at(-2), lax.rem(r + 2 * core - 1 + rows, rows))
    partner = r + 1 - 2 * core
    out_group = (1, 3, g_x_out)
    in_group = (1, 3, g_x_in)

    idx_copies = [
        send(bc_h, ridx.at[g], idx_sem.at[0, g], idx_sem.at[1, g], (row_at(OFFSETS[g]), y))
        for g in range(4)
    ]

    def rows_of(owner):
        return pl.ds(pl.multiple_of(owner * bs // Y, bs // Y), bs // Y)

    quarter_copies = [
        send(
            h_hbm.at[pl.ds(6 * g, 6), pl.ds(10, 2), rows_of(y)],
            hrem.at[g, :, :, rows_of(y)],
            h_sem.at[0, j],
            h_sem.at[1, j],
            (to_row[j], y),
        )
        for j, g in enumerate(out_group)
    ]
    chip_copy = send(
        h_hbm.at[pl.ds(6 * g_chip_out, 6), pl.ds(10, 2)],
        hrem.at[g_chip_out],
        h_sem.at[0, 3],
        h_sem.at[1, 3],
        (partner, y),
    )
    for g in range(1, 4):
        load_rows(g)

    def local_rows(current, first_row, count, unroll):
        def body(i, carry):
            b = first_row + i
            lhs = jnp.concatenate([ham[b, k] for k in range(10)], axis=1)
            rhs = jnp.concatenate(
                [vec[current, inside(bc_s[b * 12 + k])] for k in range(10)], axis=0
            )
            acc[b] = jnp.dot(lhs, rhs, preferred_element_type=F32)
            return carry

        lax.fori_loop(0, count, body, 0, unroll=unroll)

    def products(step, g):
        def body(i, carry):
            lhs = jnp.concatenate([hrem[g, i, 0], hrem[g, i, 1]], axis=1)
            rhs = jnp.concatenate(
                [
                    vec[step, inside(ridx[g, (6 * g + i) * 12 + 10 + q])]
                    for q in range(2)
                ],
                axis=0,
            )
            psend[step - 1, g, i] = jnp.dot(lhs, rhs, preferred_element_type=F32).astype(BF16)
            return carry

        lax.fori_loop(0, 6, body, 0, unroll=6)

    in_groups = (*in_group, g_chip_in)
    back_to = (row_at(-2), row_at(2), lax.rem(r + 2 * core - 1 + rows, rows), partner)

    def product_copy(step, g, h, peer):
        part = pl.ds(PER_PART * h, PER_PART)
        return (
            psend.at[step - 1, g, part],
            precv.at[step - 1, g, part],
            p_sem.at[0, step - 1, h, g],
            p_sem.at[1, step - 1, h, g],
            peer,
        )

    def send_products(step, j, h):
        send(*product_copy(step, in_groups[j], h, (back_to[j], y)))

    loaded("vec")

    def vector_copy(g, h, peer):
        part = pl.ds(2 * PER_PART * h, 2 * PER_PART)
        return (
            vsend.at[g, part],
            vrecv.at[g, part],
            v_sem.at[0, h, g],
            v_sem.at[1, h, g],
            peer,
        )

    for copy in idx_copies:
        copy.wait_recv()
    for j in (0, 1, 3, 2):
        g = in_groups[j]

        def pick(i, carry, g=g):
            for q in range(2):
                entry = inside(ridx[g, (6 * g + i) * 12 + 10 + q])
                vsend[g, 2 * i + q] = vec[0, entry]
            return carry

        lax.fori_loop(0, 6, pick, 0, unroll=2)
        for h in range(PARTS):
            send(*vector_copy(g, h, (back_to[j], y)))

    loaded(0)
    local_rows(0, 0, 6, 2)
    loaded(1)
    local_rows(0, 6, 6, 2)

    fwd = []
    for j in range(3):
        quarter_copies[j].wait_recv()
        part = hrem.at[in_group[j], :, :, rows_of(y)]
        fwd.append(
            [
                send(
                    part,
                    part,
                    fwd_sem.at[0, j, side],
                    fwd_sem.at[1, j, side],
                    (r, col_at(d)),
                )
                for side, d in enumerate((1, -1))
            ]
        )
    loaded(2)
    local_rows(0, 12, 6, 2)
    loaded(3)
    local_rows(0, 18, 6, 2)
    second = []
    for j in range(3):
        pair = []
        for side, d in enumerate((1, -1)):
            fwd[j][side].wait_recv()
            part = hrem.at[in_group[j], :, pl.ds(side, 1), rows_of(col_at(-d))]
            pair.append(
                send(
                    part,
                    part,
                    fwd_sem.at[0, j, 2 + side],
                    fwd_sem.at[1, j, 2 + side],
                    (r, col_at(d)),
                )
            )
        second.append(pair)

    def finish(step, g, h):
        args = vector_copy if step == 0 else functools.partial(product_copy, step)
        remote(*args(g, h, (partner, y))).wait_recv()

        def body(i, carry):
            b = 6 * g + PER_PART * h + i
            n = PER_PART * h + i
            if step == 0:
                product = acc[b] + jnp.dot(
                    jnp.concatenate([ham[b, 10], ham[b, 11]], axis=1),
                    jnp.concatenate([vrecv[g, 2 * n], vrecv[g, 2 * n + 1]], axis=0),
                    preferred_element_type=F32,
                )
            else:
                product = acc[b] + precv[step - 1, g, n].astype(F32)
            shifted = product - CENTER * vec[step, b].astype(F32)
            if step == 0:
                vec[1, b] = (shifted / HALF).astype(BF16)
            else:
                vec[step + 1, b] = (
                    2.0 * shifted / HALF - vec[step - 1, b].astype(F32)
                ).astype(BF16)
            return carry

        lax.fori_loop(0, PER_PART, body, 0, unroll=PER_PART)

    def to_mine(g, h, source=y, local=False):
        group = vec.at[STEPS, pl.ds(6 * g + PER_PART * h, PER_PART)]
        place = mine.at[source, pl.ds(PER_PART * h, PER_PART)]
        if local:
            return pltpu.make_async_copy(group, place, a_sem.at[1, h, y])
        return remote(group, place, a_sem.at[0, h, g], a_sem.at[1, h, source], (r, g))

    def to_hbm(g, h):
        rows_g = pl.ds(6 * g + PER_PART * h, PER_PART)
        return pltpu.make_async_copy(
            vec.at[STEPS, rows_g], f_hbm.at[rows_g], out_sem.at[h, g]
        )

    def scatter(g, h):
        @pl.when(g != y)
        def _():
            to_mine(g, h).start()

        @pl.when(g == y)
        def _():
            to_mine(g, h, local=True).start()

        to_hbm(g, h).start()

    def close_scatter():
        for h in range(PARTS):
            for d in range(1, Y):
                to_mine(col_at(d), h).wait_send()
            for g in range(4):
                to_hbm(g, h).wait()

    own_groups = (1, 3, g_x_out)
    parts = range(PARTS)
    for step in range(STEPS):

        def complete(g, h, step=step):
            finish(step, g, h)
            if step == STEPS - 1:
                scatter(g, h)

        if step > 0:
            if step == 1:
                for j in (0, 1):
                    for copy in second[j]:
                        copy.wait_recv()
                chip_copy.wait_recv()
            for j in (0, 1):
                products(step, in_groups[j])
                send_products(step, j, 0)
            products(step, g_chip_in)
            for h in parts:
                send_products(step, 3, h)
            if step == 1:
                for copy in second[2]:
                    copy.wait_recv()
            products(step, in_groups[2])
            send_products(step, 2, 0)
            for h in parts[1:]:
                for j in range(3):
                    send_products(step, j, h)
            local_rows(step, 6 * g_chip_out, 6, 6)
        for h in parts:
            complete(g_chip_out, h)
        if step > 0:
            for g in own_groups:
                local_rows(step, 6 * g, 6, 6)
        for h in parts:
            for g in own_groups:
                complete(g, h)

    for h in parts:
        to_mine(y, h, local=True).wait()
        for d in range(1, Y):
            to_mine(col_at(d), h, source=col_at(d)).wait_recv()

    depth = 6 * bs
    everything = jnp.concatenate(
        [mine[s].reshape(depth, bs) for s in range(Y)], axis=1
    )

    for i in range(Y):
        part = lax.dot_general(
            mine[i].reshape(depth, bs),
            everything,
            (((0,), (0,)), ((), ())),
            preferred_element_type=F32,
        )
        for k in range(2):
            rows_k = slice(k * bs // 2, (k + 1) * bs // 2)
            for c in range(2):
                ssum[k, c, i] = part[rows_k, c * 2 * bs : (c + 1) * 2 * bs].astype(BF16)

    def sem(k, n):
        return s_sem.at[0, k, n], s_sem.at[1, k, n]

    def far_first(size):
        return sorted(range(1, size), key=lambda d: -min(d, size - d))

    offsets = [(d, e) for d in range(Y) for e in range(X) if d or e]
    offsets.sort(key=lambda o: -min(o[0], Y - o[0]) - min(o[1], X - o[1]))
    chunks = range(2)
    copies = [
        send(ssum.at[k, 1 - core], half_recv.at[k], *sem(k, 0), (partner, y))
        for k in chunks
    ]
    after = []
    for k in chunks:
        copies[k].wait_recv()
        for i in range(Y):
            both = ssum[k, core, i].astype(F32) + half_recv[k, i].astype(F32)
            for j in range(X):
                tsum[k, i, j] = both[j * piece : (j + 1) * piece].astype(BF16)
        after.append(
            [
                send(
                    tsum.at[k, col_at(d), lax.rem(x + e, X)],
                    yx_recv.at[k, (-d % Y) * X + -e % X],
                    *sem(k, d * X + e),
                    (x_at(e, core), col_at(d)),
                )
                for d, e in offsets
            ]
        )
    copies, after = after, []
    for k in chunks:
        total = tsum[k, y, x].astype(F32)
        for copy in copies[k]:
            copy.wait_recv()
        for n in range(1, Y * X):
            total += yx_recv[k, n].astype(F32)
        zsum[k] = total.astype(BF16)
        after.append(
            [
                send(zsum.at[k], z_recv.at[k, z], *sem(k, Y * X + d), (z_at(d), y))
                for d in far_first(z_count)
            ]
        )
        z_recv[k, z] = total.astype(BF16)
    copies, after = after, []
    others = [(d, e) for d in range(X) for e in range(2) if d or e]
    for k in chunks:
        for copy in copies[k]:
            copy.wait_recv()
        total = z_recv[k, 0].astype(F32)
        for d in range(1, z_count):
            total += z_recv[k, d].astype(F32)
        final[k] = (total / norb).astype(BF16)
        after.append(
            [
                send(
                    final.at[k],
                    every.at[k, X - d if d else 0, e],
                    *sem(k, Y * X + z_count + 2 * d + e),
                    (x_at(d, lax.rem(core + e, 2)), y),
                )
                for d, e in others
            ]
        )

    def place(k, xx, c, value):
        rows_k = pl.ds(pl.multiple_of(k * bs // 2 + xx * piece, piece), piece)
        columns_c = pl.ds(pl.multiple_of(c * 2 * bs, 2 * bs), 2 * bs)
        inter[rows_k, columns_c] = value.astype(F32)

    for k in chunks:
        place(k, x, core, final[k])
    for k in chunks:
        for copy in after[k]:
            copy.wait_recv()
        for d, e in others:
            back = X - d if d else 0
            place(k, lax.rem(x + back, X), lax.rem(core + e, 2), every[k, back, e])
    close()
    close_scatter()


def on_device(hamiltonian, block_column, vectors):
    bs = hamiltonian.shape[1]
    rows = lax.axis_size("row")
    z_count = rows // (2 * X)
    ham = hamiltonian.reshape(24, 12, bs, bs)
    vec = vectors.reshape(24, bs, bs)
    dma = pltpu.SemaphoreType.DMA
    any_spec = pl.BlockSpec(memory_space=pl.ANY)
    filtered, inter = pl.pallas_call(
        functools.partial(kernel, rows, float(rows * 24 * bs)),
        out_shape=(
            jax.ShapeDtypeStruct((24, bs, bs), BF16),
            jax.ShapeDtypeStruct((bs, Y * bs), F32),
        ),
        in_specs=[pl.BlockSpec(memory_space=pltpu.SMEM), any_spec, any_spec, any_spec],
        out_specs=(any_spec, pl.BlockSpec(memory_space=pltpu.VMEM)),
        scratch_shapes=[
            pltpu.VMEM((24, 12, bs, bs), BF16),
            pltpu.VMEM((STEPS + 1, 24, bs, bs), BF16),
            pltpu.VMEM((24, bs, bs), F32),
            pltpu.VMEM((4, 6, 2, bs, bs), BF16),
            pltpu.VMEM((4, 12, bs, bs), BF16),
            pltpu.VMEM((4, 12, bs, bs), BF16),
            pltpu.VMEM((STEPS - 1, 4, 6, bs, bs), BF16),
            pltpu.VMEM((STEPS - 1, 4, 6, bs, bs), BF16),
            pltpu.SMEM((4, 288), jnp.int32),
            pltpu.VMEM((Y, 6, bs, bs), BF16),
            pltpu.VMEM((2, Y, bs // 2, 2 * bs), BF16),
            pltpu.VMEM((2, Y, X, bs // (2 * X), 2 * bs), BF16),
            pltpu.VMEM((2, Y * X, bs // (2 * X), 2 * bs), BF16),
            pltpu.VMEM((2, bs // (2 * X), 2 * bs), BF16),
            pltpu.VMEM((2, z_count, bs // (2 * X), 2 * bs), BF16),
            pltpu.VMEM((2, bs // (2 * X), 2 * bs), BF16),
            pltpu.VMEM((2, X, 2, bs // (2 * X), 2 * bs), BF16),
            pltpu.VMEM((2, 2, Y, bs // 2, 2 * bs), BF16),
            dma((5,)),
            dma((2, 4)),
            dma((2, 4)),
            dma((2, 3, 4)),
            dma((2, PARTS, 4)),
            dma((2, STEPS - 1, PARTS, 4)),
            dma((2, PARTS, 4)),
            dma((2, 2, Y * X + z_count + 2 * X)),
            dma((PARTS, 4)),
        ],
        compiler_params=pltpu.CompilerParams(
            collective_id=0, has_side_effects=True, vmem_limit_bytes=64 * 2**20 - 2**17
        ),
        name="chebyshev",
    )(block_column, block_column, ham, vec)
    return filtered.reshape(24 * bs, bs), inter


def solution(mesh):
    return jax.shard_map(
        on_device,
        mesh=mesh,
        in_specs=(P("row", None, None), P("row"), P("row", "col")),
        out_specs=(P("row", "col"), P("col", None)),
        check_vma=False,
    )
```

```python
import functools

import jax
import jax.numpy as jnp
from jax import lax
from jax.experimental import pallas as pl
from jax.experimental.pallas import tpu as pltpu
from jax.sharding import PartitionSpec as P

MESH = pl.DeviceIdType.MESH
STEPS = 3
OFFSETS = (1, 2, -1, -2)
BF16 = jnp.bfloat16
F32 = jnp.float32
CENTER = 0.2
HALF = 0.8
X = 4
Y = 4
PARTS = (1, 2, 3)
MOST = max(PARTS)
CHUNKS = 1


def kernel(
    rows,
    norb,
    bc_s,
    bc_h,
    h_hbm,
    v_hbm,
    f_hbm,
    inter,
    ham,
    vec,
    acc,
    hrem,
    vsend,
    vrecv,
    psend,
    precv,
    ridx,
    mine,
    half_recv,
    tsum,
    yx_recv,
    zsum,
    z_recv,
    final,
    every,
    ssum,
    load_sem,
    idx_sem,
    h_sem,
    fwd_sem,
    v_sem,
    p_sem,
    a_sem,
    s_sem,
    out_sem,
):
    z_count = rows // (2 * X)
    r = lax.axis_index("row")
    y = lax.axis_index("col")
    core = lax.rem(r, 2)
    x = lax.rem(r // 2, X)
    z = r // (2 * X)
    bs = ham.shape[-1]
    piece = bs // (CHUNKS * X)
    base = r * 24

    def inside(entry):
        return jnp.clip(entry - base, 0, 23)

    def row_at(offset):
        return lax.rem(r + offset + rows, rows)

    def col_at(offset):
        return lax.rem(y + offset + Y, Y)

    def x_at(offset, c):
        return z * 2 * X + lax.rem(x + offset, X) * 2 + c

    def z_at(offset):
        return lax.rem(z + offset, z_count) * 2 * X + x * 2 + core

    sends = []
    loads = {}

    def load(name, src, dst, sem):
        loads[name] = pltpu.make_async_copy(src, dst, sem)
        loads[name].start()

    def loaded(name):
        loads.pop(name).wait()

    def remote(src, dst, send_sem, recv_sem, peer):
        return pltpu.make_async_remote_copy(
            src_ref=src,
            dst_ref=dst,
            send_sem=send_sem,
            recv_sem=recv_sem,
            device_id=peer,
            device_id_type=MESH,
        )

    def send(*args):
        copy = remote(*args)
        copy.start()
        sends.append(copy)
        return copy

    def close():
        for copy in sends:
            copy.wait_send()
        for name in tuple(loads):
            loaded(name)

    load("vec", v_hbm, vec.at[0], load_sem.at[4])

    def load_rows(g):
        load(g, h_hbm.at[pl.ds(6 * g, 6)], ham.at[pl.ds(6 * g, 6)], load_sem.at[g])

    load_rows(0)

    peers = [(row_at(o), y) for o in OFFSETS]
    peers += [(r, col_at(d)) for d in range(1, Y)]
    peers += [(x_at(d, c), y) for d in range(1, X) for c in range(2)]
    peers += [(z_at(d), y) for d in range(1, z_count)]
    peers += [(x_at(d, core), col_at(e)) for d in range(1, X) for e in range(1, Y)]
    barrier = pltpu.get_barrier_semaphore()
    for peer in peers:
        pl.semaphore_signal(barrier, inc=1, device_id=peer, device_id_type=MESH)
    pl.semaphore_wait(barrier, len(peers))

    g_x_out, g_chip_out = 2 * (1 - core), 2 * core
    g_x_in, g_chip_in = 2 * core, 2 * (1 - core)
    to_row = (row_at(2), row_at(-2), lax.rem(r + 2 * core - 1 + rows, rows))
    partner = r + 1 - 2 * core
    out_group = (1, 3, g_x_out)
    in_group = (1, 3, g_x_in)

    idx_copies = [
        send(bc_h, ridx.at[g], idx_sem.at[0, g], idx_sem.at[1, g], (row_at(OFFSETS[g]), y))
        for g in range(4)
    ]

    def rows_of(owner):
        return pl.ds(pl.multiple_of(owner * bs // Y, bs // Y), bs // Y)

    quarter_copies = [
        send(
            h_hbm.at[pl.ds(6 * g, 6), pl.ds(10, 2), rows_of(y)],
            hrem.at[g, :, :, rows_of(y)],
            h_sem.at[0, j],
            h_sem.at[1, j],
            (to_row[j], y),
        )
        for j, g in enumerate(out_group)
    ]
    chip_copy = send(
        h_hbm.at[pl.ds(6 * g_chip_out, 6), pl.ds(10, 2)],
        hrem.at[g_chip_out],
        h_sem.at[0, 3],
        h_sem.at[1, 3],
        (partner, y),
    )
    for g in range(1, 4):
        load_rows(g)

    def local_rows(current, first_row, count, unroll):
        def body(i, carry):
            b = first_row + i
            lhs = jnp.concatenate([ham[b, k] for k in range(10)], axis=1)
            rhs = jnp.concatenate(
                [vec[current, inside(bc_s[b * 12 + k])] for k in range(10)], axis=0
            )
            acc[b] = jnp.dot(lhs, rhs, preferred_element_type=F32)
            return carry

        lax.fori_loop(0, count, body, 0, unroll=unroll)

    def products(step, g):
        def body(i, carry):
            lhs = jnp.concatenate([hrem[g, i, 0], hrem[g, i, 1]], axis=1)
            rhs = jnp.concatenate(
                [
                    vec[step, inside(ridx[g, (6 * g + i) * 12 + 10 + q])]
                    for q in range(2)
                ],
                axis=0,
            )
            psend[step - 1, g, i] = jnp.dot(lhs, rhs, preferred_element_type=F32).astype(BF16)
            return carry

        lax.fori_loop(0, 6, body, 0, unroll=6)

    in_groups = (*in_group, g_chip_in)
    back_to = (row_at(-2), row_at(2), lax.rem(r + 2 * core - 1 + rows, rows), partner)

    def product_copy(step, g, h, peer):
        part = part_of(step, h)
        return (
            psend.at[step - 1, g, part],
            precv.at[step - 1, g, part],
            p_sem.at[0, step - 1, h, g],
            p_sem.at[1, step - 1, h, g],
            peer,
        )

    def send_products(step, j, h):
        send(*product_copy(step, in_groups[j], h, (back_to[j], y)))

    loaded("vec")

    def part_of(step, h, each=1, first=0):
        count = 6 // PARTS[step]
        return pl.ds(first + each * count * h, each * count)

    def vector_copy(g, h, peer):
        part = part_of(0, h, 2)
        return (
            vsend.at[g, part],
            vrecv.at[g, part],
            v_sem.at[0, h, g],
            v_sem.at[1, h, g],
            peer,
        )

    for copy in idx_copies:
        copy.wait_recv()
    for j in (0, 1, 3, 2):
        g = in_groups[j]

        def pick(i, carry, g=g):
            for q in range(2):
                entry = inside(ridx[g, (6 * g + i) * 12 + 10 + q])
                vsend[g, 2 * i + q] = vec[0, entry]
            return carry

        lax.fori_loop(0, 6, pick, 0, unroll=2)
        for h in range(PARTS[0]):
            send(*vector_copy(g, h, (back_to[j], y)))

    loaded(0)
    local_rows(0, 0, 6, 2)
    loaded(1)
    local_rows(0, 6, 6, 2)

    fwd = []
    for j in range(3):
        quarter_copies[j].wait_recv()
        part = hrem.at[in_group[j], :, :, rows_of(y)]
        fwd.append(
            [
                send(
                    part,
                    part,
                    fwd_sem.at[0, j, side],
                    fwd_sem.at[1, j, side],
                    (r, col_at(d)),
                )
                for side, d in enumerate((1, -1))
            ]
        )
    loaded(2)
    local_rows(0, 12, 6, 2)
    loaded(3)
    local_rows(0, 18, 6, 2)
    second = []
    for j in range(3):
        pair = []
        for side, d in enumerate((1, -1)):
            fwd[j][side].wait_recv()
            part = hrem.at[in_group[j], :, pl.ds(side, 1), rows_of(col_at(-d))]
            pair.append(
                send(
                    part,
                    part,
                    fwd_sem.at[0, j, 2 + side],
                    fwd_sem.at[1, j, 2 + side],
                    (r, col_at(d)),
                )
            )
        second.append(pair)

    def finish(step, g, h):
        args = vector_copy if step == 0 else functools.partial(product_copy, step)
        remote(*args(g, h, (partner, y))).wait_recv()

        def body(i, carry):
            n = 6 // PARTS[step] * h + i
            b = 6 * g + n
            if step == 0:
                product = acc[b] + jnp.dot(
                    jnp.concatenate([ham[b, 10], ham[b, 11]], axis=1),
                    jnp.concatenate([vrecv[g, 2 * n], vrecv[g, 2 * n + 1]], axis=0),
                    preferred_element_type=F32,
                )
            else:
                product = acc[b] + precv[step - 1, g, n].astype(F32)
            shifted = product - CENTER * vec[step, b].astype(F32)
            if step == 0:
                vec[1, b] = (shifted / HALF).astype(BF16)
            else:
                vec[step + 1, b] = (
                    2.0 * shifted / HALF - vec[step - 1, b].astype(F32)
                ).astype(BF16)
            return carry

        lax.fori_loop(0, 6 // PARTS[step], body, 0, unroll=2 if PARTS[step] == 3 else 3)

    def to_mine(g, h, source=y, local=False):
        group = vec.at[STEPS, part_of(-1, h, first=6 * g)]
        place = mine.at[source, part_of(-1, h)]
        if local:
            return pltpu.make_async_copy(group, place, a_sem.at[1, h, y])
        return remote(group, place, a_sem.at[0, h, g], a_sem.at[1, h, source], (r, g))

    to_hbm = pltpu.make_async_copy(vec.at[STEPS], f_hbm, out_sem)

    def scatter(g, h):
        @pl.when(g != y)
        def _():
            to_mine(g, h).start()

        @pl.when(g == y)
        def _():
            to_mine(g, h, local=True).start()

    def close_scatter():
        for h in range(PARTS[-1]):
            for d in range(1, Y):
                to_mine(col_at(d), h).wait_send()
        to_hbm.wait()

    own_groups = (1, 3, g_x_out)
    for step in range(STEPS):
        parts = range(PARTS[step])

        def complete(g, h, step=step):
            finish(step, g, h)
            if step == STEPS - 1:
                scatter(g, h)

        if step > 0:
            if step == 1:
                for j in (0, 1):
                    for copy in second[j]:
                        copy.wait_recv()
                chip_copy.wait_recv()
            for j in (0, 1):
                products(step, in_groups[j])
                send_products(step, j, 0)
            products(step, g_chip_in)
            for h in parts:
                send_products(step, 3, h)
            if step == 1:
                for copy in second[2]:
                    copy.wait_recv()
            products(step, in_groups[2])
            send_products(step, 2, 0)
            for h in parts[1:]:
                for j in range(3):
                    send_products(step, j, h)
            local_rows(step, 6 * g_chip_out, 6, 6)
        for h in parts:
            complete(g_chip_out, h)
        if step > 0:
            for g in own_groups:
                local_rows(step, 6 * g, 6, 6)
        for h in parts:
            for g in own_groups:
                complete(g, h)

    to_hbm.start()
    for h in range(PARTS[-1]):
        to_mine(y, h, local=True).wait()
        for d in range(1, Y):
            to_mine(col_at(d), h, source=col_at(d)).wait_recv()

    depth = 6 * bs
    everything = jnp.concatenate(
        [mine[s].reshape(depth, bs) for s in range(Y)], axis=1
    )

    for i in range(Y):
        part = lax.dot_general(
            mine[i].reshape(depth, bs),
            everything,
            (((0,), (0,)), ((), ())),
            preferred_element_type=F32,
        )
        for k in range(CHUNKS):
            rows_k = slice(k * bs // CHUNKS, (k + 1) * bs // CHUNKS)
            for c in range(2):
                ssum[k, c, i] = part[rows_k, c * 2 * bs : (c + 1) * 2 * bs].astype(BF16)

    def sem(k, n):
        return s_sem.at[0, k, n], s_sem.at[1, k, n]

    def far_first(size):
        return sorted(range(1, size), key=lambda d: -min(d, size - d))

    offsets = [(d, e) for d in range(Y) for e in range(X) if d or e]
    offsets.sort(key=lambda o: -min(o[0], Y - o[0]) - min(o[1], X - o[1]))
    chunks = range(CHUNKS)
    copies = [
        send(ssum.at[k, 1 - core], half_recv.at[k], *sem(k, 0), (partner, y))
        for k in chunks
    ]
    after = []
    for k in chunks:
        copies[k].wait_recv()
        for i in range(Y):
            both = ssum[k, core, i].astype(F32) + half_recv[k, i].astype(F32)
            for j in range(X):
                tsum[k, i, j] = both[j * piece : (j + 1) * piece].astype(BF16)
        after.append(
            [
                send(
                    tsum.at[k, col_at(d), lax.rem(x + e, X)],
                    yx_recv.at[k, (-d % Y) * X + -e % X],
                    *sem(k, d * X + e),
                    (x_at(e, core), col_at(d)),
                )
                for d, e in offsets
            ]
        )
    copies, after = after, []
    for k in chunks:
        total = tsum[k, y, x].astype(F32)
        for copy in copies[k]:
            copy.wait_recv()
        for n in range(1, Y * X):
            total += yx_recv[k, n].astype(F32)
        zsum[k] = total.astype(BF16)
        after.append(
            [
                send(zsum.at[k], z_recv.at[k, z], *sem(k, Y * X + d), (z_at(d), y))
                for d in far_first(z_count)
            ]
        )
        z_recv[k, z] = total.astype(BF16)
    copies, after = after, []
    others = [(d, e) for d in range(X) for e in range(2) if d or e]
    for k in chunks:
        for copy in copies[k]:
            copy.wait_recv()
        total = z_recv[k, 0].astype(F32)
        for d in range(1, z_count):
            total += z_recv[k, d].astype(F32)
        final[k] = (total / norb).astype(BF16)
        after.append(
            [
                send(
                    final.at[k],
                    every.at[k, X - d if d else 0, e],
                    *sem(k, Y * X + z_count + 2 * d + e),
                    (x_at(d, lax.rem(core + e, 2)), y),
                )
                for d, e in others
            ]
        )

    def place(k, xx, c, value):
        rows_k = pl.ds(pl.multiple_of(k * bs // CHUNKS + xx * piece, piece), piece)
        columns_c = pl.ds(pl.multiple_of(c * 2 * bs, 2 * bs), 2 * bs)
        inter[rows_k, columns_c] = value.astype(F32)

    for k in chunks:
        place(k, x, core, final[k])
    for k in chunks:
        for copy in after[k]:
            copy.wait_recv()
        for d, e in others:
            back = X - d if d else 0
            place(k, lax.rem(x + back, X), lax.rem(core + e, 2), every[k, back, e])
    close()
    close_scatter()


def publish(f_from, inter_from, f_to, inter_to, f_held, inter_held, copy_sem):
    pairs = [(f_from, f_held), (inter_from, inter_held), (f_held, f_to), (inter_held, inter_to)]
    copies = [
        pltpu.make_async_copy(src, dst, copy_sem.at[n]) for n, (src, dst) in enumerate(pairs)
    ]
    for n in (0, 1):
        copies[n].start()
    for n in (0, 1):
        copies[n].wait()
        copies[2 + n].start()
    for n in (2, 3):
        copies[n].wait()


def on_device(hamiltonian, block_column, vectors):
    bs = hamiltonian.shape[1]
    rows = lax.axis_size("row")
    z_count = rows // (2 * X)
    piece = bs // (CHUNKS * X)
    ham = hamiltonian.reshape(24, 12, bs, bs)
    vec = vectors.reshape(24, bs, bs)
    dma = pltpu.SemaphoreType.DMA
    any_spec = pl.BlockSpec(memory_space=pl.ANY)
    filtered, inter = pl.pallas_call(
        functools.partial(kernel, rows, float(rows * 24 * bs)),
        out_shape=(
            jax.ShapeDtypeStruct((24, bs, bs), BF16),
            jax.ShapeDtypeStruct((bs, Y * bs), F32),
        ),
        in_specs=[pl.BlockSpec(memory_space=pltpu.SMEM), any_spec, any_spec, any_spec],
        out_specs=(any_spec, pl.BlockSpec(memory_space=pltpu.VMEM)),
        scratch_shapes=[
            pltpu.VMEM((24, 12, bs, bs), BF16),
            pltpu.VMEM((STEPS + 1, 24, bs, bs), BF16),
            pltpu.VMEM((24, bs, bs), F32),
            pltpu.VMEM((4, 6, 2, bs, bs), BF16),
            pltpu.VMEM((4, 12, bs, bs), BF16),
            pltpu.VMEM((4, 12, bs, bs), BF16),
            pltpu.VMEM((STEPS - 1, 4, 6, bs, bs), BF16),
            pltpu.VMEM((STEPS - 1, 4, 6, bs, bs), BF16),
            pltpu.SMEM((4, 288), jnp.int32),
            pltpu.VMEM((Y, 6, bs, bs), BF16),
            pltpu.VMEM((CHUNKS, Y, bs // CHUNKS, 2 * bs), BF16),
            pltpu.VMEM((CHUNKS, Y, X, piece, 2 * bs), BF16),
            pltpu.VMEM((CHUNKS, Y * X, piece, 2 * bs), BF16),
            pltpu.VMEM((CHUNKS, piece, 2 * bs), BF16),
            pltpu.VMEM((CHUNKS, z_count, piece, 2 * bs), BF16),
            pltpu.VMEM((CHUNKS, piece, 2 * bs), BF16),
            pltpu.VMEM((CHUNKS, X, 2, piece, 2 * bs), BF16),
            pltpu.VMEM((CHUNKS, 2, Y, bs // CHUNKS, 2 * bs), BF16),
            dma((5,)),
            dma((2, 4)),
            dma((2, 4)),
            dma((2, 3, 4)),
            dma((2, MOST, 4)),
            dma((2, STEPS - 1, MOST, 4)),
            dma((2, MOST, 4)),
            dma((2, CHUNKS, Y * X + z_count + 2 * X)),
            dma,
        ],
        compiler_params=pltpu.CompilerParams(
            collective_id=0, has_side_effects=True, vmem_limit_bytes=64 * 2**20 - 2**17
        ),
        name="chebyshev",
    )(block_column, block_column, ham, vec)
    filtered, inter = pl.pallas_call(
        publish,
        out_shape=(
            jax.ShapeDtypeStruct((24, bs, bs), BF16),
            jax.ShapeDtypeStruct((bs, Y * bs), F32),
        ),
        in_specs=[any_spec] * 2,
        out_specs=(any_spec, any_spec),
        scratch_shapes=[
            pltpu.VMEM((24, bs, bs), BF16),
            pltpu.VMEM((bs, Y * bs), F32),
            dma((4,)),
        ],
        compiler_params=pltpu.CompilerParams(vmem_limit_bytes=64 * 2**20 - 2**17),
        name="publish",
    )(filtered, inter)
    return filtered.reshape(24 * bs, bs), inter


def solution(mesh):
    return jax.shard_map(
        on_device,
        mesh=mesh,
        in_specs=(P("row", None, None), P("row"), P("row", "col")),
        out_specs=(P("row", "col"), P("col", None)),
        check_vma=False,
    )
```

```python
import functools

import jax
import jax.numpy as jnp
from jax import lax
from jax.experimental import pallas as pl
from jax.experimental.pallas import tpu as pltpu
from jax.sharding import PartitionSpec as P

MESH = pl.DeviceIdType.MESH
STEPS = 3
OFFSETS = (1, 2, -1, -2)
BF16 = jnp.bfloat16
F32 = jnp.float32
CENTER = 0.2
HALF = 0.8
X = 4
Y = 4
PARTS = (1, 1, 3)
MOST = max(PARTS)
CHUNKS = 1


def kernel(
    rows,
    norb,
    bc_s,
    bc_h,
    h_hbm,
    v_hbm,
    f_hbm,
    inter,
    ham,
    vec,
    acc,
    hrem,
    vsend,
    vrecv,
    psend,
    precv,
    ridx,
    mine,
    half_recv,
    tsum,
    yx_recv,
    zsum,
    z_recv,
    final,
    every,
    ssum,
    load_sem,
    idx_sem,
    h_sem,
    fwd_sem,
    v_sem,
    p_sem,
    a_sem,
    s_sem,
    out_sem,
):
    z_count = rows // (2 * X)
    r = lax.axis_index("row")
    y = lax.axis_index("col")
    core = lax.rem(r, 2)
    x = lax.rem(r // 2, X)
    z = r // (2 * X)
    bs = ham.shape[-1]
    piece = bs // (CHUNKS * X)
    base = r * 24

    def inside(entry):
        return jnp.clip(entry - base, 0, 23)

    def row_at(offset):
        return lax.rem(r + offset + rows, rows)

    def col_at(offset):
        return lax.rem(y + offset + Y, Y)

    def x_at(offset, c):
        return z * 2 * X + lax.rem(x + offset, X) * 2 + c

    def z_at(offset):
        return lax.rem(z + offset, z_count) * 2 * X + x * 2 + core

    sends = []
    loads = {}

    def load(name, src, dst, sem):
        loads[name] = pltpu.make_async_copy(src, dst, sem)
        loads[name].start()

    def loaded(name):
        loads.pop(name).wait()

    def remote(src, dst, send_sem, recv_sem, peer):
        return pltpu.make_async_remote_copy(
            src_ref=src,
            dst_ref=dst,
            send_sem=send_sem,
            recv_sem=recv_sem,
            device_id=peer,
            device_id_type=MESH,
        )

    def send(*args):
        copy = remote(*args)
        copy.start()
        sends.append(copy)
        return copy

    def drain(count=None):
        done = sends[:count]
        del sends[:count]
        for copy in done:
            copy.wait_send()

    def close():
        drain()
        for name in tuple(loads):
            loaded(name)

    peers = [(row_at(o), y) for o in OFFSETS]
    peers += [(r, col_at(d)) for d in range(1, Y)]
    peers += [(x_at(d, c), y) for d in range(1, X) for c in range(2)]
    peers += [(z_at(d), y) for d in range(1, z_count)]
    peers += [(x_at(d, core), col_at(e)) for d in range(1, X) for e in range(1, Y)]
    barrier = pltpu.get_barrier_semaphore()
    for peer in peers:
        pl.semaphore_signal(barrier, inc=1, device_id=peer, device_id_type=MESH)
    load("vec", v_hbm, vec.at[0], load_sem.at[4])

    def load_rows(g):
        load(g, h_hbm.at[pl.ds(6 * g, 6)], ham.at[pl.ds(6 * g, 6)], load_sem.at[g])

    load_rows(0)
    pl.semaphore_wait(barrier, len(peers))

    g_x_out, g_chip_out = 2 * (1 - core), 2 * core
    g_x_in, g_chip_in = 2 * core, 2 * (1 - core)
    to_row = (row_at(2), row_at(-2), lax.rem(r + 2 * core - 1 + rows, rows))
    partner = r + 1 - 2 * core
    out_group = (1, 3, g_x_out)
    in_group = (1, 3, g_x_in)

    idx_copies = [
        send(bc_h, ridx.at[g], idx_sem.at[0, g], idx_sem.at[1, g], (row_at(OFFSETS[g]), y))
        for g in range(4)
    ]

    def rows_of(owner):
        return pl.ds(pl.multiple_of(owner * bs // Y, bs // Y), bs // Y)

    quarter_copies = [
        send(
            h_hbm.at[pl.ds(6 * g, 6), pl.ds(10, 2), rows_of(y)],
            hrem.at[g, :, :, rows_of(y)],
            h_sem.at[0, j],
            h_sem.at[1, j],
            (to_row[j], y),
        )
        for j, g in enumerate(out_group)
    ]
    chip_copy = send(
        h_hbm.at[pl.ds(6 * g_chip_out, 6), pl.ds(10, 2)],
        hrem.at[g_chip_out],
        h_sem.at[0, 3],
        h_sem.at[1, 3],
        (partner, y),
    )
    for g in range(1, 4):
        load_rows(g)

    def local_rows(current, first_row, count, unroll):
        def body(i, carry):
            b = first_row + i
            lhs = jnp.concatenate([ham[b, k] for k in range(10)], axis=1)
            rhs = jnp.concatenate(
                [vec[current, inside(bc_s[b * 12 + k])] for k in range(10)], axis=0
            )
            acc[b] = jnp.dot(lhs, rhs, preferred_element_type=F32)
            return carry

        lax.fori_loop(0, count, body, 0, unroll=unroll)

    def products(step, g):
        def body(i, carry):
            lhs = jnp.concatenate([hrem[g, i, 0], hrem[g, i, 1]], axis=1)
            rhs = jnp.concatenate(
                [
                    vec[step, inside(ridx[g, (6 * g + i) * 12 + 10 + q])]
                    for q in range(2)
                ],
                axis=0,
            )
            psend[step - 1, g, i] = jnp.dot(lhs, rhs, preferred_element_type=F32).astype(BF16)
            return carry

        lax.fori_loop(0, 6, body, 0, unroll=6)

    in_groups = (*in_group, g_chip_in)
    back_to = (row_at(-2), row_at(2), lax.rem(r + 2 * core - 1 + rows, rows), partner)

    def product_copy(step, g, h, peer):
        part = part_of(step, h)
        return (
            psend.at[step - 1, g, part],
            precv.at[step - 1, g, part],
            p_sem.at[0, step - 1, h, g],
            p_sem.at[1, step - 1, h, g],
            peer,
        )

    def send_products(step, j, h):
        send(*product_copy(step, in_groups[j], h, (back_to[j], y)))

    loaded("vec")

    def part_of(step, h, each=1, first=0):
        count = 6 // PARTS[step]
        return pl.ds(first + each * count * h, each * count)

    def vector_copy(g, h, peer):
        part = part_of(0, h, 2)
        return (
            vsend.at[g, part],
            vrecv.at[g, part],
            v_sem.at[0, h, g],
            v_sem.at[1, h, g],
            peer,
        )

    for copy in idx_copies:
        copy.wait_recv()
    for j in (0, 1, 3, 2):
        g = in_groups[j]

        def pick(i, carry, g=g):
            for q in range(2):
                entry = inside(ridx[g, (6 * g + i) * 12 + 10 + q])
                vsend[g, 2 * i + q] = vec[0, entry]
            return carry

        lax.fori_loop(0, 6, pick, 0, unroll=2)
        for h in range(PARTS[0]):
            send(*vector_copy(g, h, (back_to[j], y)))

    loaded(0)
    local_rows(0, 0, 6, 2)
    loaded(1)
    local_rows(0, 6, 6, 2)

    fwd = []
    for j in range(3):
        quarter_copies[j].wait_recv()
        part = hrem.at[in_group[j], :, :, rows_of(y)]
        fwd.append(
            [
                send(
                    part,
                    part,
                    fwd_sem.at[0, j, side],
                    fwd_sem.at[1, j, side],
                    (r, col_at(d)),
                )
                for side, d in enumerate((1, -1))
            ]
        )
    loaded(2)
    local_rows(0, 12, 6, 2)
    loaded(3)
    local_rows(0, 18, 6, 2)
    second = []
    for j in range(3):
        pair = []
        for side, d in enumerate((1, -1)):
            fwd[j][side].wait_recv()
            part = hrem.at[in_group[j], :, pl.ds(side, 1), rows_of(col_at(-d))]
            pair.append(
                send(
                    part,
                    part,
                    fwd_sem.at[0, j, 2 + side],
                    fwd_sem.at[1, j, 2 + side],
                    (r, col_at(d)),
                )
            )
        second.append(pair)

    def finish(step, g, h):
        args = vector_copy if step == 0 else functools.partial(product_copy, step)
        remote(*args(g, h, (partner, y))).wait_recv()

        def body(i, carry):
            n = 6 // PARTS[step] * h + i
            b = 6 * g + n
            if step == 0:
                product = acc[b] + jnp.dot(
                    jnp.concatenate([ham[b, 10], ham[b, 11]], axis=1),
                    jnp.concatenate([vrecv[g, 2 * n], vrecv[g, 2 * n + 1]], axis=0),
                    preferred_element_type=F32,
                )
            else:
                product = acc[b] + precv[step - 1, g, n].astype(F32)
            shifted = product - CENTER * vec[step, b].astype(F32)
            if step == 0:
                vec[1, b] = (shifted / HALF).astype(BF16)
            else:
                vec[step + 1, b] = (
                    2.0 * shifted / HALF - vec[step - 1, b].astype(F32)
                ).astype(BF16)
            return carry

        lax.fori_loop(0, 6 // PARTS[step], body, 0, unroll=2 if PARTS[step] == 3 else 3)

    def to_mine(g, h, source=y, local=False):
        group = vec.at[STEPS, part_of(-1, h, first=6 * g)]
        place = mine.at[source, part_of(-1, h)]
        if local:
            return pltpu.make_async_copy(group, place, a_sem.at[1, h, y])
        return remote(group, place, a_sem.at[0, h, g], a_sem.at[1, h, source], (r, g))

    to_hbm = pltpu.make_async_copy(vec.at[STEPS], f_hbm, out_sem)

    def scatter(g, h):
        @pl.when(g != y)
        def _():
            to_mine(g, h).start()

        @pl.when(g == y)
        def _():
            to_mine(g, h, local=True).start()

    def close_scatter():
        for h in range(PARTS[-1]):
            for d in range(1, Y):
                to_mine(col_at(d), h).wait_send()

    own_groups = (1, 3, g_x_out)
    for step in range(STEPS):
        parts = range(PARTS[step])
        before = len(sends) if step else 8

        def complete(g, h, step=step):
            finish(step, g, h)
            if step == STEPS - 1:
                scatter(g, h)

        if step > 0:
            if step == 1:
                for j in (0, 1):
                    for copy in second[j]:
                        copy.wait_recv()
                chip_copy.wait_recv()
            for j in (0, 1):
                products(step, in_groups[j])
                send_products(step, j, 0)
            products(step, g_chip_in)
            for h in parts:
                send_products(step, 3, h)
            if step == 1:
                for copy in second[2]:
                    copy.wait_recv()
            products(step, in_groups[2])
            send_products(step, 2, 0)
            for h in parts[1:]:
                for j in range(3):
                    send_products(step, j, h)
            local_rows(step, 6 * g_chip_out, 6, 6)
        for h in parts:
            complete(g_chip_out, h)
        if step > 0:
            for g in own_groups:
                local_rows(step, 6 * g, 6, 6)
        drain(before)
        for h in parts:
            for g in own_groups:
                complete(g, h)

    to_hbm.start()
    drain()
    for h in range(PARTS[-1]):
        to_mine(y, h, local=True).wait()
        for d in range(1, Y):
            to_mine(col_at(d), h, source=col_at(d)).wait_recv()

    depth = 6 * bs
    everything = jnp.concatenate(
        [mine[s].reshape(depth, bs) for s in range(Y)], axis=1
    )

    for i in range(Y):
        part = lax.dot_general(
            mine[i].reshape(depth, bs),
            everything,
            (((0,), (0,)), ((), ())),
            preferred_element_type=F32,
        )
        for k in range(CHUNKS):
            rows_k = slice(k * bs // CHUNKS, (k + 1) * bs // CHUNKS)
            for c in range(2):
                ssum[k, c, i] = part[rows_k, c * 2 * bs : (c + 1) * 2 * bs].astype(BF16)

    def sem(k, n):
        return s_sem.at[0, k, n], s_sem.at[1, k, n]

    def far_first(size):
        return sorted(range(1, size), key=lambda d: -min(d, size - d))

    offsets = [(d, e) for d in range(Y) for e in range(X) if d or e]
    offsets.sort(key=lambda o: -min(o[0], Y - o[0]) - min(o[1], X - o[1]))
    chunks = range(CHUNKS)
    copies = [
        send(ssum.at[k, 1 - core], half_recv.at[k], *sem(k, 0), (partner, y))
        for k in chunks
    ]
    after = []
    for k in chunks:
        copies[k].wait_recv()
        for i in range(Y):
            both = ssum[k, core, i].astype(F32) + half_recv[k, i].astype(F32)
            for j in range(X):
                tsum[k, i, j] = both[j * piece : (j + 1) * piece].astype(BF16)
        after.append(
            [
                send(
                    tsum.at[k, col_at(d), lax.rem(x + e, X)],
                    yx_recv.at[k, (-d % Y) * X + -e % X],
                    *sem(k, d * X + e),
                    (x_at(e, core), col_at(d)),
                )
                for d, e in offsets
            ]
        )
    close_scatter()
    copies, after = after, []
    for k in chunks:
        total = tsum[k, y, x].astype(F32)
        for copy in copies[k]:
            copy.wait_recv()
        for n in range(1, Y * X):
            total += yx_recv[k, n].astype(F32)
        zsum[k] = total.astype(BF16)
        after.append(
            [
                send(zsum.at[k], z_recv.at[k, z], *sem(k, Y * X + d), (z_at(d), y))
                for d in far_first(z_count)
            ]
        )
        z_recv[k, z] = total.astype(BF16)
    drain(1 + len(offsets) * CHUNKS)
    copies, after = after, []
    others = [(d, e) for d in range(X) for e in range(2) if d or e]
    for k in chunks:
        for copy in copies[k]:
            copy.wait_recv()
        total = z_recv[k, 0].astype(F32)
        for d in range(1, z_count):
            total += z_recv[k, d].astype(F32)
        final[k] = (total / norb).astype(BF16)
        after.append(
            [
                send(
                    final.at[k],
                    every.at[k, X - d if d else 0, e],
                    *sem(k, Y * X + z_count + 2 * d + e),
                    (x_at(d, lax.rem(core + e, 2)), y),
                )
                for d, e in others
            ]
        )

    def place(k, xx, c, value):
        rows_k = pl.ds(pl.multiple_of(k * bs // CHUNKS + xx * piece, piece), piece)
        columns_c = pl.ds(pl.multiple_of(c * 2 * bs, 2 * bs), 2 * bs)
        inter[rows_k, columns_c] = value.astype(F32)

    for k in chunks:
        place(k, x, core, final[k])
    drain((z_count - 1) * CHUNKS)
    to_hbm.wait()
    for k in chunks:
        for copy in after[k]:
            copy.wait_recv()
        for d, e in others:
            back = X - d if d else 0
            place(k, lax.rem(x + back, X), lax.rem(core + e, 2), every[k, back, e])
    close()


def publish(f_from, inter_from, f_to, inter_to, f_held, inter_held, copy_sem):
    halves = [pl.ds(0, 12), pl.ds(12, 12)]
    arrays = [(f_from.at[h], f_held.at[h], f_to.at[h]) for h in halves]
    arrays.append((inter_from, inter_held, inter_to))
    inward = [
        pltpu.make_async_copy(a, b, copy_sem.at[0, n]) for n, (a, b, _) in enumerate(arrays)
    ]
    outward = [
        pltpu.make_async_copy(b, c, copy_sem.at[1, n]) for n, (_, b, c) in enumerate(arrays)
    ]
    for copy in inward:
        copy.start()
    for first, then in zip(inward, outward):
        first.wait()
        then.start()
    for copy in outward:
        copy.wait()


def on_device(hamiltonian, block_column, vectors):
    bs = hamiltonian.shape[1]
    rows = lax.axis_size("row")
    z_count = rows // (2 * X)
    piece = bs // (CHUNKS * X)
    ham = hamiltonian.reshape(24, 12, bs, bs)
    vec = vectors.reshape(24, bs, bs)
    dma = pltpu.SemaphoreType.DMA
    any_spec = pl.BlockSpec(memory_space=pl.ANY)
    filtered, inter = pl.pallas_call(
        functools.partial(kernel, rows, float(rows * 24 * bs)),
        out_shape=(
            jax.ShapeDtypeStruct((24, bs, bs), BF16),
            jax.ShapeDtypeStruct((bs, Y * bs), F32),
        ),
        in_specs=[pl.BlockSpec(memory_space=pltpu.SMEM), any_spec, any_spec, any_spec],
        out_specs=(any_spec, pl.BlockSpec(memory_space=pltpu.VMEM)),
        scratch_shapes=[
            pltpu.VMEM((24, 12, bs, bs), BF16),
            pltpu.VMEM((STEPS + 1, 24, bs, bs), BF16),
            pltpu.VMEM((24, bs, bs), F32),
            pltpu.VMEM((4, 6, 2, bs, bs), BF16),
            pltpu.VMEM((4, 12, bs, bs), BF16),
            pltpu.VMEM((4, 12, bs, bs), BF16),
            pltpu.VMEM((STEPS - 1, 4, 6, bs, bs), BF16),
            pltpu.VMEM((STEPS - 1, 4, 6, bs, bs), BF16),
            pltpu.SMEM((4, 288), jnp.int32),
            pltpu.VMEM((Y, 6, bs, bs), BF16),
            pltpu.VMEM((CHUNKS, Y, bs // CHUNKS, 2 * bs), BF16),
            pltpu.VMEM((CHUNKS, Y, X, piece, 2 * bs), BF16),
            pltpu.VMEM((CHUNKS, Y * X, piece, 2 * bs), BF16),
            pltpu.VMEM((CHUNKS, piece, 2 * bs), BF16),
            pltpu.VMEM((CHUNKS, z_count, piece, 2 * bs), BF16),
            pltpu.VMEM((CHUNKS, piece, 2 * bs), BF16),
            pltpu.VMEM((CHUNKS, X, 2, piece, 2 * bs), BF16),
            pltpu.VMEM((CHUNKS, 2, Y, bs // CHUNKS, 2 * bs), BF16),
            dma((5,)),
            dma((2, 4)),
            dma((2, 4)),
            dma((2, 3, 4)),
            dma((2, MOST, 4)),
            dma((2, STEPS - 1, MOST, 4)),
            dma((2, MOST, 4)),
            dma((2, CHUNKS, Y * X + z_count + 2 * X)),
            dma,
        ],
        compiler_params=pltpu.CompilerParams(
            collective_id=0, has_side_effects=True, vmem_limit_bytes=64 * 2**20 - 2**17
        ),
        name="chebyshev",
    )(block_column, block_column, ham, vec)
    filtered, inter = pl.pallas_call(
        publish,
        out_shape=(
            jax.ShapeDtypeStruct((24, bs, bs), BF16),
            jax.ShapeDtypeStruct((bs, Y * bs), F32),
        ),
        in_specs=[any_spec] * 2,
        out_specs=(any_spec, any_spec),
        scratch_shapes=[
            pltpu.VMEM((24, bs, bs), BF16),
            pltpu.VMEM((bs, Y * bs), F32),
            dma((2, 3)),
        ],
        compiler_params=pltpu.CompilerParams(vmem_limit_bytes=64 * 2**20 - 2**17),
        name="publish",
    )(filtered, inter)
    return filtered.reshape(24 * bs, bs), inter


def solution(mesh):
    return jax.shard_map(
        on_device,
        mesh=mesh,
        in_specs=(P("row", None, None), P("row"), P("row", "col")),
        out_specs=(P("row", "col"), P("col", None)),
        check_vma=False,
    )
```

```python
import functools

import jax
import jax.numpy as jnp
from jax import lax
from jax.experimental import pallas as pl
from jax.experimental.pallas import tpu as pltpu
from jax.sharding import PartitionSpec as P

MESH = pl.DeviceIdType.MESH
STEPS = 3
OFFSETS = (1, 2, -1, -2)
BF16 = jnp.bfloat16
F32 = jnp.float32
CENTER = 0.2
HALF = 0.8
X = 4
Y = 4
PARTS = (1, 1, 3)
MOST = max(PARTS)
CHUNKS = 1


def kernel(
    rows,
    norb,
    bc_s,
    bc_h,
    h_hbm,
    v_hbm,
    f_hbm,
    inter,
    ham,
    vec,
    acc,
    hrem,
    vsend,
    vrecv,
    psend,
    precv,
    ridx,
    mine,
    half_recv,
    tsum,
    yx_recv,
    zsum,
    z_recv,
    final,
    every,
    ssum,
    load_sem,
    idx_sem,
    h_sem,
    fwd_sem,
    v_sem,
    p_sem,
    a_sem,
    s_sem,
    out_sem,
):
    z_count = rows // (2 * X)
    r = lax.axis_index("row")
    y = lax.axis_index("col")
    core = lax.rem(r, 2)
    x = lax.rem(r // 2, X)
    z = r // (2 * X)
    bs = ham.shape[-1]
    piece = bs // (CHUNKS * X)
    base = r * 24

    def inside(entry):
        return jnp.clip(entry - base, 0, 23)

    def row_at(offset):
        return lax.rem(r + offset + rows, rows)

    def col_at(offset):
        return lax.rem(y + offset + Y, Y)

    def x_at(offset, c):
        return z * 2 * X + lax.rem(x + offset, X) * 2 + c

    def z_at(offset):
        return lax.rem(z + offset, z_count) * 2 * X + x * 2 + core

    sends = []
    loads = {}

    def load(name, src, dst, sem):
        loads[name] = pltpu.make_async_copy(src, dst, sem)
        loads[name].start()

    def loaded(name):
        loads.pop(name).wait()

    def remote(src, dst, send_sem, recv_sem, peer):
        return pltpu.make_async_remote_copy(
            src_ref=src,
            dst_ref=dst,
            send_sem=send_sem,
            recv_sem=recv_sem,
            device_id=peer,
            device_id_type=MESH,
        )

    def send(*args):
        copy = remote(*args)
        copy.start()
        sends.append(copy)
        return copy

    def drain(count=None):
        done = sends[:count]
        del sends[:count]
        for copy in done:
            copy.wait_send()

    def close():
        drain()
        for name in tuple(loads):
            loaded(name)

    peers = [(row_at(o), y) for o in OFFSETS]
    peers += [(r, col_at(d)) for d in range(1, Y)]
    peers += [(x_at(d, c), y) for d in range(1, X) for c in range(2)]
    peers += [(z_at(d), y) for d in range(1, z_count)]
    peers += [(x_at(d, core), col_at(e)) for d in range(1, X) for e in range(1, Y)]
    barrier = pltpu.get_barrier_semaphore()
    for peer in peers:
        pl.semaphore_signal(barrier, inc=1, device_id=peer, device_id_type=MESH)
    load("vec", v_hbm, vec.at[0], load_sem.at[4])

    def load_rows(g):
        load(g, h_hbm.at[pl.ds(6 * g, 6)], ham.at[pl.ds(6 * g, 6)], load_sem.at[g])

    load_rows(0)
    pl.semaphore_wait(barrier, len(peers))

    g_x_out, g_chip_out = 2 * (1 - core), 2 * core
    g_x_in, g_chip_in = 2 * core, 2 * (1 - core)
    to_row = (row_at(2), row_at(-2), lax.rem(r + 2 * core - 1 + rows, rows))
    partner = r + 1 - 2 * core
    out_group = (1, 3, g_x_out)
    in_group = (1, 3, g_x_in)

    idx_copies = [
        send(bc_h, ridx.at[g], idx_sem.at[0, g], idx_sem.at[1, g], (row_at(OFFSETS[g]), y))
        for g in range(4)
    ]

    def rows_of(owner):
        return pl.ds(pl.multiple_of(owner * bs // Y, bs // Y), bs // Y)

    quarter_copies = [
        send(
            h_hbm.at[pl.ds(6 * g, 6), pl.ds(10, 2), rows_of(y)],
            hrem.at[g, :, :, rows_of(y)],
            h_sem.at[0, j],
            h_sem.at[1, j],
            (to_row[j], y),
        )
        for j, g in enumerate(out_group)
    ]
    chip_copy = send(
        h_hbm.at[pl.ds(6 * g_chip_out, 6), pl.ds(10, 2)],
        hrem.at[g_chip_out],
        h_sem.at[0, 3],
        h_sem.at[1, 3],
        (partner, y),
    )
    for g in range(1, 4):
        load_rows(g)

    def scale(step):
        return (2.0 if step else 1.0) / HALF

    def local_rows(current, first_row, count, unroll):
        def body(i, carry):
            b = first_row + i
            lhs = jnp.concatenate([ham[b, k] for k in range(10)], axis=1)
            rhs = jnp.concatenate(
                [vec[current, inside(bc_s[b * 12 + k])] for k in range(10)], axis=0
            )
            product = jnp.dot(lhs, rhs, preferred_element_type=F32)
            shifted = scale(current) * (product - CENTER * vec[current, b].astype(F32))
            if current > 0:
                shifted = shifted - vec[current - 1, b].astype(F32)
            acc[b] = shifted
            return carry

        lax.fori_loop(0, count, body, 0, unroll=unroll)

    def products(step, g):
        def body(i, carry):
            lhs = jnp.concatenate([hrem[g, i, 0], hrem[g, i, 1]], axis=1)
            rhs = jnp.concatenate(
                [
                    vec[step, inside(ridx[g, (6 * g + i) * 12 + 10 + q])]
                    for q in range(2)
                ],
                axis=0,
            )
            psend[step - 1, g, i] = jnp.dot(lhs, rhs, preferred_element_type=F32).astype(BF16)
            return carry

        lax.fori_loop(0, 6, body, 0, unroll=6)

    in_groups = (*in_group, g_chip_in)
    back_to = (row_at(-2), row_at(2), lax.rem(r + 2 * core - 1 + rows, rows), partner)

    def product_copy(step, g, h, peer):
        part = part_of(step, h)
        return (
            psend.at[step - 1, g, part],
            precv.at[step - 1, g, part],
            p_sem.at[0, step - 1, h, g],
            p_sem.at[1, step - 1, h, g],
            peer,
        )

    def send_products(step, j, h):
        send(*product_copy(step, in_groups[j], h, (back_to[j], y)))

    loaded("vec")

    def part_of(step, h, each=1, first=0):
        count = 6 // PARTS[step]
        return pl.ds(first + each * count * h, each * count)

    def vector_copy(g, h, peer):
        part = part_of(0, h, 2)
        return (
            vsend.at[g, part],
            vrecv.at[g, part],
            v_sem.at[0, h, g],
            v_sem.at[1, h, g],
            peer,
        )

    for copy in idx_copies:
        copy.wait_recv()
    for j in (0, 1, 3, 2):
        g = in_groups[j]

        def pick(i, carry, g=g):
            for q in range(2):
                entry = inside(ridx[g, (6 * g + i) * 12 + 10 + q])
                vsend[g, 2 * i + q] = vec[0, entry]
            return carry

        lax.fori_loop(0, 6, pick, 0, unroll=2)
        for h in range(PARTS[0]):
            send(*vector_copy(g, h, (back_to[j], y)))

    loaded(0)
    local_rows(0, 0, 6, 2)
    loaded(1)
    local_rows(0, 6, 6, 2)

    fwd = []
    for j in range(3):
        quarter_copies[j].wait_recv()
        part = hrem.at[in_group[j], :, :, rows_of(y)]
        fwd.append(
            [
                send(
                    part,
                    part,
                    fwd_sem.at[0, j, side],
                    fwd_sem.at[1, j, side],
                    (r, col_at(d)),
                )
                for side, d in enumerate((1, -1))
            ]
        )
    loaded(2)
    local_rows(0, 12, 6, 2)
    loaded(3)
    local_rows(0, 18, 6, 2)
    second = []
    for j in range(3):
        pair = []
        for side, d in enumerate((1, -1)):
            fwd[j][side].wait_recv()
            part = hrem.at[in_group[j], :, pl.ds(side, 1), rows_of(col_at(-d))]
            pair.append(
                send(
                    part,
                    part,
                    fwd_sem.at[0, j, 2 + side],
                    fwd_sem.at[1, j, 2 + side],
                    (r, col_at(d)),
                )
            )
        second.append(pair)

    def finish(step, g, h):
        args = vector_copy if step == 0 else functools.partial(product_copy, step)
        remote(*args(g, h, (partner, y))).wait_recv()

        def body(i, carry):
            n = 6 // PARTS[step] * h + i
            b = 6 * g + n
            if step == 0:
                product = jnp.dot(
                    jnp.concatenate([ham[b, 10], ham[b, 11]], axis=1),
                    jnp.concatenate([vrecv[g, 2 * n], vrecv[g, 2 * n + 1]], axis=0),
                    preferred_element_type=F32,
                )
            else:
                product = precv[step - 1, g, n].astype(F32)
            vec[step + 1, b] = (acc[b] + scale(step) * product).astype(BF16)
            return carry

        lax.fori_loop(0, 6 // PARTS[step], body, 0, unroll=2 if PARTS[step] == 3 else 3)

    def to_mine(g, h, source=y, local=False):
        group = vec.at[STEPS, part_of(-1, h, first=6 * g)]
        place = mine.at[source, part_of(-1, h)]
        if local:
            return pltpu.make_async_copy(group, place, a_sem.at[1, h, y])
        return remote(group, place, a_sem.at[0, h, g], a_sem.at[1, h, source], (r, g))

    to_hbm = pltpu.make_async_copy(vec.at[STEPS], f_hbm, out_sem)

    def scatter(g, h):
        @pl.when(g != y)
        def _():
            to_mine(g, h).start()

        @pl.when(g == y)
        def _():
            to_mine(g, h, local=True).start()

    def close_scatter():
        for h in range(PARTS[-1]):
            for d in range(1, Y):
                to_mine(col_at(d), h).wait_send()

    own_groups = (1, 3, g_x_out)
    for step in range(STEPS):
        parts = range(PARTS[step])
        before = len(sends) if step else 8

        def complete(g, h, step=step):
            finish(step, g, h)
            if step == STEPS - 1:
                scatter(g, h)

        if step > 0:
            if step == 1:
                for j in (0, 1):
                    for copy in second[j]:
                        copy.wait_recv()
                chip_copy.wait_recv()
            for j in (0, 1):
                products(step, in_groups[j])
                send_products(step, j, 0)
            products(step, g_chip_in)
            for h in parts:
                send_products(step, 3, h)
            if step == 1:
                for copy in second[2]:
                    copy.wait_recv()
            products(step, in_groups[2])
            send_products(step, 2, 0)
            for h in parts[1:]:
                for j in range(3):
                    send_products(step, j, h)
            local_rows(step, 6 * g_chip_out, 6, 6)
        for h in parts:
            complete(g_chip_out, h)
        if step > 0:
            for g in own_groups:
                local_rows(step, 6 * g, 6, 6)
        drain(before)
        for h in parts:
            for g in own_groups:
                complete(g, h)

    to_hbm.start()
    drain()
    for h in range(PARTS[-1]):
        to_mine(y, h, local=True).wait()
        for d in range(1, Y):
            to_mine(col_at(d), h, source=col_at(d)).wait_recv()

    depth = 6 * bs

    def sums(c):
        columns = jnp.concatenate(
            [mine[2 * c + s].reshape(depth, bs) for s in range(2)], axis=1
        )
        for i in range(Y):
            part = lax.dot_general(
                mine[i].reshape(depth, bs),
                columns,
                (((0,), (0,)), ((), ())),
                preferred_element_type=F32,
            )
            for k in range(CHUNKS):
                rows_k = slice(k * bs // CHUNKS, (k + 1) * bs // CHUNKS)
                ssum[k, c, i] = part[rows_k].astype(BF16)

    sums(1 - core)

    def sem(k, n):
        return s_sem.at[0, k, n], s_sem.at[1, k, n]

    def far_first(size):
        return sorted(range(1, size), key=lambda d: -min(d, size - d))

    offsets = [(d, e) for d in range(Y) for e in range(X) if d or e]
    offsets.sort(key=lambda o: -min(o[0], Y - o[0]) - min(o[1], X - o[1]))
    chunks = range(CHUNKS)
    copies = [
        send(ssum.at[k, 1 - core], half_recv.at[k], *sem(k, 0), (partner, y))
        for k in chunks
    ]
    sums(core)
    after = []
    for k in chunks:
        copies[k].wait_recv()
        for i in range(Y):
            both = ssum[k, core, i].astype(F32) + half_recv[k, i].astype(F32)
            for j in range(X):
                tsum[k, i, j] = both[j * piece : (j + 1) * piece].astype(BF16)
        after.append(
            [
                send(
                    tsum.at[k, col_at(d), lax.rem(x + e, X)],
                    yx_recv.at[k, (-d % Y) * X + -e % X],
                    *sem(k, d * X + e),
                    (x_at(e, core), col_at(d)),
                )
                for d, e in offsets
            ]
        )
    close_scatter()
    copies, after = after, []
    for k in chunks:
        total = tsum[k, y, x].astype(F32)
        for copy in copies[k]:
            copy.wait_recv()
        for n in range(1, Y * X):
            total += yx_recv[k, n].astype(F32)
        zsum[k] = total.astype(BF16)
        after.append(
            [
                send(zsum.at[k], z_recv.at[k, z], *sem(k, Y * X + d), (z_at(d), y))
                for d in far_first(z_count)
            ]
        )
        z_recv[k, z] = total.astype(BF16)
    drain(1 + len(offsets) * CHUNKS)
    copies, after = after, []
    others = [(d, e) for d in range(X) for e in range(2) if d or e]
    for k in chunks:
        for copy in copies[k]:
            copy.wait_recv()
        total = z_recv[k, 0].astype(F32)
        for d in range(1, z_count):
            total += z_recv[k, d].astype(F32)
        final[k] = (total / norb).astype(BF16)
        after.append(
            [
                send(
                    final.at[k],
                    every.at[k, X - d if d else 0, e],
                    *sem(k, Y * X + z_count + 2 * d + e),
                    (x_at(d, lax.rem(core + e, 2)), y),
                )
                for d, e in others
            ]
        )

    def place(k, xx, c, value):
        rows_k = pl.ds(pl.multiple_of(k * bs // CHUNKS + xx * piece, piece), piece)
        columns_c = pl.ds(pl.multiple_of(c * 2 * bs, 2 * bs), 2 * bs)
        inter[rows_k, columns_c] = value.astype(F32)

    for k in chunks:
        place(k, x, core, final[k])
    drain((z_count - 1) * CHUNKS)
    to_hbm.wait()
    for k in chunks:
        for copy in after[k]:
            copy.wait_recv()
        for d, e in others:
            back = X - d if d else 0
            place(k, lax.rem(x + back, X), lax.rem(core + e, 2), every[k, back, e])
    close()


def publish(f_from, inter_from, f_to, inter_to, f_held, inter_held, copy_sem):
    halves = [pl.ds(0, 12), pl.ds(12, 12)]
    arrays = [(f_from.at[h], f_held.at[h], f_to.at[h]) for h in halves]
    arrays.append((inter_from, inter_held, inter_to))
    inward = [
        pltpu.make_async_copy(a, b, copy_sem.at[0, n]) for n, (a, b, _) in enumerate(arrays)
    ]
    outward = [
        pltpu.make_async_copy(b, c, copy_sem.at[1, n]) for n, (_, b, c) in enumerate(arrays)
    ]
    for copy in inward:
        copy.start()
    for first, then in zip(inward, outward):
        first.wait()
        then.start()
    for copy in outward:
        copy.wait()


def on_device(hamiltonian, block_column, vectors):
    bs = hamiltonian.shape[1]
    rows = lax.axis_size("row")
    z_count = rows // (2 * X)
    piece = bs // (CHUNKS * X)
    ham = hamiltonian.reshape(24, 12, bs, bs)
    vec = vectors.reshape(24, bs, bs)
    dma = pltpu.SemaphoreType.DMA
    any_spec = pl.BlockSpec(memory_space=pl.ANY)
    filtered, inter = pl.pallas_call(
        functools.partial(kernel, rows, float(rows * 24 * bs)),
        out_shape=(
            jax.ShapeDtypeStruct((24, bs, bs), BF16),
            jax.ShapeDtypeStruct((bs, Y * bs), F32),
        ),
        in_specs=[pl.BlockSpec(memory_space=pltpu.SMEM), any_spec, any_spec, any_spec],
        out_specs=(any_spec, pl.BlockSpec(memory_space=pltpu.VMEM)),
        scratch_shapes=[
            pltpu.VMEM((24, 12, bs, bs), BF16),
            pltpu.VMEM((STEPS + 1, 24, bs, bs), BF16),
            pltpu.VMEM((24, bs, bs), F32),
            pltpu.VMEM((4, 6, 2, bs, bs), BF16),
            pltpu.VMEM((4, 12, bs, bs), BF16),
            pltpu.VMEM((4, 12, bs, bs), BF16),
            pltpu.VMEM((STEPS - 1, 4, 6, bs, bs), BF16),
            pltpu.VMEM((STEPS - 1, 4, 6, bs, bs), BF16),
            pltpu.SMEM((4, 288), jnp.int32),
            pltpu.VMEM((Y, 6, bs, bs), BF16),
            pltpu.VMEM((CHUNKS, Y, bs // CHUNKS, 2 * bs), BF16),
            pltpu.VMEM((CHUNKS, Y, X, piece, 2 * bs), BF16),
            pltpu.VMEM((CHUNKS, Y * X, piece, 2 * bs), BF16),
            pltpu.VMEM((CHUNKS, piece, 2 * bs), BF16),
            pltpu.VMEM((CHUNKS, z_count, piece, 2 * bs), BF16),
            pltpu.VMEM((CHUNKS, piece, 2 * bs), BF16),
            pltpu.VMEM((CHUNKS, X, 2, piece, 2 * bs), BF16),
            pltpu.VMEM((CHUNKS, 2, Y, bs // CHUNKS, 2 * bs), BF16),
            dma((5,)),
            dma((2, 4)),
            dma((2, 4)),
            dma((2, 3, 4)),
            dma((2, MOST, 4)),
            dma((2, STEPS - 1, MOST, 4)),
            dma((2, MOST, 4)),
            dma((2, CHUNKS, Y * X + z_count + 2 * X)),
            dma,
        ],
        compiler_params=pltpu.CompilerParams(
            collective_id=0, has_side_effects=True, vmem_limit_bytes=53 * 2**20
        ),
        name="chebyshev",
    )(block_column, block_column, ham, vec)
    filtered, inter = pl.pallas_call(
        publish,
        out_shape=(
            jax.ShapeDtypeStruct((24, bs, bs), BF16),
            jax.ShapeDtypeStruct((bs, Y * bs), F32),
        ),
        in_specs=[any_spec] * 2,
        out_specs=(any_spec, any_spec),
        scratch_shapes=[
            pltpu.VMEM((24, bs, bs), BF16),
            pltpu.VMEM((bs, Y * bs), F32),
            dma((2, 3)),
        ],
        compiler_params=pltpu.CompilerParams(vmem_limit_bytes=53 * 2**20),
        name="publish",
    )(filtered, inter)
    return filtered.reshape(24 * bs, bs), inter


def solution(mesh):
    return jax.shard_map(
        on_device,
        mesh=mesh,
        in_specs=(P("row", None, None), P("row"), P("row", "col")),
        out_specs=(P("row", "col"), P("col", None)),
        check_vma=False,
    )
```

```python
import functools

import jax
import jax.numpy as jnp
from jax import lax
from jax.experimental import pallas as pl
from jax.experimental.pallas import tpu as pltpu
from jax.sharding import PartitionSpec as P

MESH = pl.DeviceIdType.MESH
STEPS = 3
OFFSETS = (1, 2, -1, -2)
BF16 = jnp.bfloat16
F32 = jnp.float32
CENTER = 0.2
HALF = 0.8
X = 4
Y = 4
PARTS = (1, 1, 2)
MOST = max(PARTS)
CHUNKS = 1


def kernel(
    rows,
    norb,
    bc_s,
    bc_h,
    h_hbm,
    v_hbm,
    f_hbm,
    inter,
    ham,
    vec,
    acc,
    hrem,
    vsend,
    vrecv,
    psend,
    precv,
    ridx,
    mine,
    half_recv,
    tsum,
    yx_recv,
    zsum,
    z_recv,
    final,
    every,
    ssum,
    load_sem,
    idx_sem,
    h_sem,
    fwd_sem,
    v_sem,
    p_sem,
    a_sem,
    s_sem,
    out_sem,
):
    z_count = rows // (2 * X)
    r = lax.axis_index("row")
    y = lax.axis_index("col")
    core = lax.rem(r, 2)
    x = lax.rem(r // 2, X)
    z = r // (2 * X)
    bs = ham.shape[-1]
    piece = bs // (CHUNKS * X)
    base = r * 24

    def inside(entry):
        return jnp.clip(entry - base, 0, 23)

    def row_at(offset):
        return lax.rem(r + offset + rows, rows)

    def col_at(offset):
        return lax.rem(y + offset + Y, Y)

    def x_at(offset, c):
        return z * 2 * X + lax.rem(x + offset, X) * 2 + c

    def z_at(offset):
        return lax.rem(z + offset, z_count) * 2 * X + x * 2 + core

    sends = []
    loads = {}

    def load(name, src, dst, sem):
        loads[name] = pltpu.make_async_copy(src, dst, sem)
        loads[name].start()

    def loaded(name):
        loads.pop(name).wait()

    def remote(src, dst, send_sem, recv_sem, peer):
        return pltpu.make_async_remote_copy(
            src_ref=src,
            dst_ref=dst,
            send_sem=send_sem,
            recv_sem=recv_sem,
            device_id=peer,
            device_id_type=MESH,
        )

    def send(*args):
        copy = remote(*args)
        copy.start()
        sends.append(copy)
        return copy

    def drain(count=None):
        done = sends[:count]
        del sends[:count]
        for copy in done:
            copy.wait_send()

    def close():
        drain()
        for name in tuple(loads):
            loaded(name)

    peers = [(row_at(o), y) for o in OFFSETS]
    peers += [(r, col_at(d)) for d in range(1, Y)]
    peers += [(x_at(d, c), y) for d in range(1, X) for c in range(2)]
    peers += [(z_at(d), y) for d in range(1, z_count)]
    peers += [(x_at(d, core), col_at(e)) for d in range(1, X) for e in range(1, Y)]
    barrier = pltpu.get_barrier_semaphore()
    for peer in peers:
        pl.semaphore_signal(barrier, inc=1, device_id=peer, device_id_type=MESH)
    load("vec", v_hbm, vec.at[0], load_sem.at[4])

    def load_rows(g):
        load(g, h_hbm.at[pl.ds(6 * g, 6)], ham.at[pl.ds(6 * g, 6)], load_sem.at[g])

    load_rows(0)
    pl.semaphore_wait(barrier, len(peers))

    g_x_out, g_chip_out = 2 * (1 - core), 2 * core
    g_x_in, g_chip_in = 2 * core, 2 * (1 - core)
    to_row = (row_at(2), row_at(-2), lax.rem(r + 2 * core - 1 + rows, rows))
    partner = r + 1 - 2 * core
    out_group = (1, 3, g_x_out)
    in_group = (1, 3, g_x_in)

    idx_copies = [
        send(bc_h, ridx.at[g], idx_sem.at[0, g], idx_sem.at[1, g], (row_at(OFFSETS[g]), y))
        for g in range(4)
    ]

    def rows_of(owner):
        return pl.ds(pl.multiple_of(owner * bs // Y, bs // Y), bs // Y)

    quarter_copies = [
        send(
            h_hbm.at[pl.ds(6 * g, 6), pl.ds(10, 2), rows_of(y)],
            hrem.at[g, :, :, rows_of(y)],
            h_sem.at[0, j],
            h_sem.at[1, j],
            (to_row[j], y),
        )
        for j, g in enumerate(out_group)
    ]
    chip_copy = send(
        h_hbm.at[pl.ds(6 * g_chip_out, 6), pl.ds(10, 2)],
        hrem.at[g_chip_out],
        h_sem.at[0, 3],
        h_sem.at[1, 3],
        (partner, y),
    )
    for g in range(1, 4):
        load_rows(g)

    def scale(step):
        return (2.0 if step else 1.0) / HALF

    def local_rows(current, first_row, count, unroll):
        def body(i, carry):
            b = first_row + i
            lhs = jnp.concatenate([ham[b, k] for k in range(10)], axis=1)
            rhs = jnp.concatenate(
                [vec[current, inside(bc_s[b * 12 + k])] for k in range(10)], axis=0
            )
            product = jnp.dot(lhs, rhs, preferred_element_type=F32)
            shifted = scale(current) * (product - CENTER * vec[current, b].astype(F32))
            if current > 0:
                shifted = shifted - vec[current - 1, b].astype(F32)
            acc[b] = shifted
            return carry

        lax.fori_loop(0, count, body, 0, unroll=unroll)

    def products(step, g):
        def body(i, carry):
            lhs = jnp.concatenate([hrem[g, i, 0], hrem[g, i, 1]], axis=1)
            rhs = jnp.concatenate(
                [
                    vec[step, inside(ridx[g, (6 * g + i) * 12 + 10 + q])]
                    for q in range(2)
                ],
                axis=0,
            )
            psend[step - 1, g, i] = jnp.dot(lhs, rhs, preferred_element_type=F32).astype(BF16)
            return carry

        lax.fori_loop(0, 6, body, 0, unroll=6)

    in_groups = (*in_group, g_chip_in)
    back_to = (row_at(-2), row_at(2), lax.rem(r + 2 * core - 1 + rows, rows), partner)

    def product_copy(step, g, h, peer):
        part = part_of(step, h)
        return (
            psend.at[step - 1, g, part],
            precv.at[step - 1, g, part],
            p_sem.at[0, step - 1, h, g],
            p_sem.at[1, step - 1, h, g],
            peer,
        )

    def send_products(step, j, h):
        send(*product_copy(step, in_groups[j], h, (back_to[j], y)))

    loaded("vec")

    def part_of(step, h, each=1, first=0):
        count = 6 // PARTS[step]
        return pl.ds(first + each * count * h, each * count)

    def vector_copy(g, h, peer):
        part = part_of(0, h, 2)
        return (
            vsend.at[g, part],
            vrecv.at[g, part],
            v_sem.at[0, h, g],
            v_sem.at[1, h, g],
            peer,
        )

    for copy in idx_copies:
        copy.wait_recv()
    for j in (0, 1, 3, 2):
        g = in_groups[j]

        def pick(i, carry, g=g):
            for q in range(2):
                entry = inside(ridx[g, (6 * g + i) * 12 + 10 + q])
                vsend[g, 2 * i + q] = vec[0, entry]
            return carry

        lax.fori_loop(0, 6, pick, 0, unroll=2)
        for h in range(PARTS[0]):
            send(*vector_copy(g, h, (back_to[j], y)))

    second = []
    for j in range(3):
        quarter_copies[j].wait_recv()
        part = hrem.at[in_group[j], :, :, rows_of(y)]
        second.append(
            [
                send(
                    part, part, fwd_sem.at[0, j, d], fwd_sem.at[1, j, d], (r, col_at(d))
                )
                for d in (2, 1, 3)
            ]
        )
    loaded(0)
    local_rows(0, 0, 6, 2)
    loaded(1)
    local_rows(0, 6, 6, 2)
    loaded(2)
    local_rows(0, 12, 6, 2)
    loaded(3)
    local_rows(0, 18, 6, 2)

    def finish(step, g, h):
        args = vector_copy if step == 0 else functools.partial(product_copy, step)
        remote(*args(g, h, (partner, y))).wait_recv()

        def body(i, carry):
            n = 6 // PARTS[step] * h + i
            b = 6 * g + n
            if step == 0:
                product = jnp.dot(
                    jnp.concatenate([ham[b, 10], ham[b, 11]], axis=1),
                    jnp.concatenate([vrecv[g, 2 * n], vrecv[g, 2 * n + 1]], axis=0),
                    preferred_element_type=F32,
                )
            else:
                product = precv[step - 1, g, n].astype(F32)
            vec[step + 1, b] = (acc[b] + scale(step) * product).astype(BF16)
            return carry

        lax.fori_loop(0, 6 // PARTS[step], body, 0, unroll=2 if PARTS[step] == 3 else 3)

    def to_mine(g, h, source=y, local=False):
        group = vec.at[STEPS, part_of(-1, h, first=6 * g)]
        place = mine.at[source, part_of(-1, h)]
        if local:
            return pltpu.make_async_copy(group, place, a_sem.at[1, h, y])
        return remote(group, place, a_sem.at[0, h, g], a_sem.at[1, h, source], (r, g))

    to_hbm = pltpu.make_async_copy(vec.at[STEPS], f_hbm, out_sem)

    def scatter(g, h):
        @pl.when(g != y)
        def _():
            to_mine(g, h).start()

        @pl.when(g == y)
        def _():
            to_mine(g, h, local=True).start()

    def close_scatter():
        for h in range(PARTS[-1]):
            for d in range(1, Y):
                to_mine(col_at(d), h).wait_send()

    own_groups = (1, 3, g_x_out)
    for step in range(STEPS):
        parts = range(PARTS[step])
        before = len(sends) if step else 8

        def complete(g, h, step=step):
            finish(step, g, h)
            if step == STEPS - 1:
                scatter(g, h)

        if step > 0:
            if step == 1:
                for j in (0, 1):
                    for copy in second[j]:
                        copy.wait_recv()
                chip_copy.wait_recv()
            for j in (0, 1):
                products(step, in_groups[j])
                send_products(step, j, 0)
            products(step, g_chip_in)
            for h in parts:
                send_products(step, 3, h)
            if step == 1:
                for copy in second[2]:
                    copy.wait_recv()
            products(step, in_groups[2])
            send_products(step, 2, 0)
            for h in parts[1:]:
                for j in range(3):
                    send_products(step, j, h)
            local_rows(step, 6 * g_chip_out, 6, 6)
        for h in parts:
            complete(g_chip_out, h)
        if step > 0:
            for g in own_groups:
                local_rows(step, 6 * g, 6, 6)
        drain(before)
        for h in parts:
            for g in own_groups:
                complete(g, h)

    to_hbm.start()
    drain()
    for h in range(PARTS[-1]):
        to_mine(y, h, local=True).wait()
        for d in range(1, Y):
            to_mine(col_at(d), h, source=col_at(d)).wait_recv()

    depth = 6 * bs

    def sums(c):
        columns = jnp.concatenate(
            [mine[2 * c + s].reshape(depth, bs) for s in range(2)], axis=1
        )
        for i in range(Y):
            part = lax.dot_general(
                mine[i].reshape(depth, bs),
                columns,
                (((0,), (0,)), ((), ())),
                preferred_element_type=F32,
            )
            for k in range(CHUNKS):
                rows_k = slice(k * bs // CHUNKS, (k + 1) * bs // CHUNKS)
                ssum[k, c, i] = part[rows_k].astype(BF16)

    sums(1 - core)

    def sem(k, n):
        return s_sem.at[0, k, n], s_sem.at[1, k, n]

    def far_first(size):
        return sorted(range(1, size), key=lambda d: -min(d, size - d))

    offsets = [(d, e) for d in range(Y) for e in range(X) if d or e]
    offsets.sort(key=lambda o: -min(o[0], Y - o[0]) - min(o[1], X - o[1]))
    chunks = range(CHUNKS)
    copies = [
        send(ssum.at[k, 1 - core], half_recv.at[k], *sem(k, 0), (partner, y))
        for k in chunks
    ]
    sums(core)
    after = []
    for k in chunks:
        copies[k].wait_recv()
        for i in range(Y):
            both = ssum[k, core, i].astype(F32) + half_recv[k, i].astype(F32)
            for j in range(X):
                tsum[k, i, j] = both[j * piece : (j + 1) * piece].astype(BF16)
        after.append(
            [
                send(
                    tsum.at[k, col_at(d), lax.rem(x + e, X)],
                    yx_recv.at[k, (-d % Y) * X + -e % X],
                    *sem(k, d * X + e),
                    (x_at(e, core), col_at(d)),
                )
                for d, e in offsets
            ]
        )
    close_scatter()
    copies, after = after, []
    for k in chunks:
        total = tsum[k, y, x].astype(F32)
        for copy in copies[k]:
            copy.wait_recv()
        for n in range(1, Y * X):
            total += yx_recv[k, n].astype(F32)
        zsum[k] = total.astype(BF16)
        after.append(
            [
                send(zsum.at[k], z_recv.at[k, z], *sem(k, Y * X + d), (z_at(d), y))
                for d in far_first(z_count)
            ]
        )
        z_recv[k, z] = total.astype(BF16)
    drain(1 + len(offsets) * CHUNKS)
    copies, after = after, []
    others = [(d, e) for d in range(X) for e in range(2) if d or e]
    for k in chunks:
        for copy in copies[k]:
            copy.wait_recv()
        total = z_recv[k, 0].astype(F32)
        for d in range(1, z_count):
            total += z_recv[k, d].astype(F32)
        final[k] = (total / norb).astype(BF16)
        after.append(
            [
                send(
                    final.at[k],
                    every.at[k, X - d if d else 0, e],
                    *sem(k, Y * X + z_count + 2 * d + e),
                    (x_at(d, lax.rem(core + e, 2)), y),
                )
                for d, e in others
            ]
        )

    def place(k, xx, c, value):
        rows_k = pl.ds(pl.multiple_of(k * bs // CHUNKS + xx * piece, piece), piece)
        columns_c = pl.ds(pl.multiple_of(c * 2 * bs, 2 * bs), 2 * bs)
        inter[rows_k, columns_c] = value.astype(F32)

    for k in chunks:
        place(k, x, core, final[k])
    drain((z_count - 1) * CHUNKS)
    to_hbm.wait()
    for k in chunks:
        for copy in after[k]:
            copy.wait_recv()
        for d, e in others:
            back = X - d if d else 0
            place(k, lax.rem(x + back, X), lax.rem(core + e, 2), every[k, back, e])
    close()


def publish(f_from, inter_from, f_to, inter_to, f_held, inter_held, copy_sem):
    halves = [pl.ds(0, 12), pl.ds(12, 12)]
    arrays = [(f_from.at[h], f_held.at[h], f_to.at[h]) for h in halves]
    arrays.append((inter_from, inter_held, inter_to))
    inward = [
        pltpu.make_async_copy(a, b, copy_sem.at[0, n]) for n, (a, b, _) in enumerate(arrays)
    ]
    outward = [
        pltpu.make_async_copy(b, c, copy_sem.at[1, n]) for n, (_, b, c) in enumerate(arrays)
    ]
    for copy in inward:
        copy.start()
    for first, then in zip(inward, outward):
        first.wait()
        then.start()
    for copy in outward:
        copy.wait()


def on_device(hamiltonian, block_column, vectors):
    bs = hamiltonian.shape[1]
    rows = lax.axis_size("row")
    z_count = rows // (2 * X)
    piece = bs // (CHUNKS * X)
    ham = hamiltonian.reshape(24, 12, bs, bs)
    vec = vectors.reshape(24, bs, bs)
    dma = pltpu.SemaphoreType.DMA
    any_spec = pl.BlockSpec(memory_space=pl.ANY)
    filtered, inter = pl.pallas_call(
        functools.partial(kernel, rows, float(rows * 24 * bs)),
        out_shape=(
            jax.ShapeDtypeStruct((24, bs, bs), BF16),
            jax.ShapeDtypeStruct((bs, Y * bs), F32),
        ),
        in_specs=[pl.BlockSpec(memory_space=pltpu.SMEM), any_spec, any_spec, any_spec],
        out_specs=(any_spec, pl.BlockSpec(memory_space=pltpu.VMEM)),
        scratch_shapes=[
            pltpu.VMEM((24, 12, bs, bs), BF16),
            pltpu.VMEM((STEPS + 1, 24, bs, bs), BF16),
            pltpu.VMEM((24, bs, bs), F32),
            pltpu.VMEM((4, 6, 2, bs, bs), BF16),
            pltpu.VMEM((4, 12, bs, bs), BF16),
            pltpu.VMEM((4, 12, bs, bs), BF16),
            pltpu.VMEM((STEPS - 1, 4, 6, bs, bs), BF16),
            pltpu.VMEM((STEPS - 1, 4, 6, bs, bs), BF16),
            pltpu.SMEM((4, 288), jnp.int32),
            pltpu.VMEM((Y, 6, bs, bs), BF16),
            pltpu.VMEM((CHUNKS, Y, bs // CHUNKS, 2 * bs), BF16),
            pltpu.VMEM((CHUNKS, Y, X, piece, 2 * bs), BF16),
            pltpu.VMEM((CHUNKS, Y * X, piece, 2 * bs), BF16),
            pltpu.VMEM((CHUNKS, piece, 2 * bs), BF16),
            pltpu.VMEM((CHUNKS, z_count, piece, 2 * bs), BF16),
            pltpu.VMEM((CHUNKS, piece, 2 * bs), BF16),
            pltpu.VMEM((CHUNKS, X, 2, piece, 2 * bs), BF16),
            pltpu.VMEM((CHUNKS, 2, Y, bs // CHUNKS, 2 * bs), BF16),
            dma((5,)),
            dma((2, 4)),
            dma((2, 4)),
            dma((2, 3, 4)),
            dma((2, MOST, 4)),
            dma((2, STEPS - 1, MOST, 4)),
            dma((2, MOST, 4)),
            dma((2, CHUNKS, Y * X + z_count + 2 * X)),
            dma,
        ],
        compiler_params=pltpu.CompilerParams(
            collective_id=0, has_side_effects=True, vmem_limit_bytes=53 * 2**20
        ),
        name="chebyshev",
    )(block_column, block_column, ham, vec)
    filtered, inter = pl.pallas_call(
        publish,
        out_shape=(
            jax.ShapeDtypeStruct((24, bs, bs), BF16),
            jax.ShapeDtypeStruct((bs, Y * bs), F32),
        ),
        in_specs=[any_spec] * 2,
        out_specs=(any_spec, any_spec),
        scratch_shapes=[
            pltpu.VMEM((24, bs, bs), BF16),
            pltpu.VMEM((bs, Y * bs), F32),
            dma((2, 3)),
        ],
        compiler_params=pltpu.CompilerParams(vmem_limit_bytes=53 * 2**20),
        name="publish",
    )(filtered, inter)
    return filtered.reshape(24 * bs, bs), inter


def solution(mesh):
    return jax.shard_map(
        on_device,
        mesh=mesh,
        in_specs=(P("row", None, None), P("row"), P("row", "col")),
        out_specs=(P("row", "col"), P("col", None)),
        check_vma=False,
    )
```
